128 devices in a mesh: wide: 16 (over x, y), pair: 8 (over z, core).
Axes of the slice: x: 4, y: 4, z: 4, core: 2. Of those that a mesh axis runs over, the one named last changes fastest.
Arguments:
- embeddings: float32 [65536, 1024], P(('wide', 'pair')), may hold values from -24 to 24
- cluster_ids: int32 [65536], P(('wide', 'pair')), may hold values from 0 to 15, as said below
Outputs:
- best_match: float32 [65536], P(('wide', 'pair'))
The draws below stay inside these ranges and needn't reach their ends.
Inputs may be any that keep to these rules, and one draw needn't show every extreme that they name: `cluster_ids`: the owner of cluster c is c. Among the 512 rows of one device, at most 64 name clusters of any one owner, and on every device some owner has exactly 64.
All inputs are finite; a program needn't handle non-finite values.
Results may differ from the reference program's by a relative error of at most 0.0003.
Values may be sent and summed in bfloat16 or wider, within the bound.
No kernel may reach another device: no remote copies, remote signals or barrier semaphores. Data moves between devices by JAX's collectives and lax.ppermute only.
A program may use at most 64 MiB of HBM per device.

```python
import math
import jax
import jax.numpy as jnp
from jax import lax

D = 1024
ROWS_DEV = 512
CL_OWN = 1
CAP = 64
CLUSTERS = 16
ROWS = 65536
N_WIDE = 16
DEVICES = 128


def cluster_rows(key):
    key = jax.random.fold_in(key, 101)
    device_keys = jax.random.split(key, DEVICES)
    slot_total = N_WIDE * CAP

    def one_device(device_key):
        first_key, score_key, shuffle_key, within_key = jax.random.split(device_key, 4)
        favored = jax.random.randint(first_key, (), 0, N_WIDE)
        slot_range = jnp.arange(slot_total, dtype=jnp.int32)
        slot_owner = slot_range // CAP
        scores = jax.random.randint(score_key, (slot_total,), 1, 2 ** 18) * slot_total + slot_range
        scores = jnp.where(slot_owner == favored, slot_range, scores)
        picked = jnp.argsort(scores, stable=True)[:ROWS_DEV].astype(jnp.int32)
        owner_list = picked // CAP
        owner_list = owner_list[jax.random.permutation(shuffle_key, ROWS_DEV)]
        within = jax.random.randint(within_key, (ROWS_DEV,), 0, CL_OWN)
        return (owner_list * CL_OWN + within).astype(jnp.int32)
    return jax.vmap(one_device)(device_keys).reshape(-1)


def draw_cluster_ids(key, part):
    return cluster_rows(key)


def draw_embeddings(key, part):
    shared_ids = cluster_rows(key)
    key = jax.random.fold_in(key, 7)
    noise_key, center_key, weight_key = jax.random.split(key, 3)
    centers = jax.random.truncated_normal(center_key, -4.0, 4.0, (CLUSTERS, D), jnp.float32)
    weights = jnp.exp(jax.random.uniform(weight_key, (ROWS, 1), jnp.float32, math.log(0.1), math.log(4.0)))
    noise = jax.random.truncated_normal(noise_key, -6.0, 6.0, (ROWS, D), jnp.float32)
    return noise + weights * centers[shared_ids]


def setup_inputs(seed: int = 0) -> dict:
    key_list = jax.random.split(jax.random.key(seed), 3)
    embeddings = draw_embeddings(jax.random.fold_in(key_list[2], 71), 0)
    cluster_ids = draw_cluster_ids(jax.random.fold_in(key_list[2], 71), 0)
    return dict(embeddings=embeddings, cluster_ids=cluster_ids)


EPSILON = 1e-06

def unit_rows(values):
    return (values * lax.rsqrt(lax.optimization_barrier(jnp.sum(values * values, axis=1, keepdims=True)) + EPSILON)).astype(jnp.bfloat16)

def reference(embeddings, cluster_ids):
    tile_span = 256
    unit = unit_rows(embeddings)
    sort_order = jnp.argsort(cluster_ids, stable=True).astype(jnp.int32)
    sorted_ids = cluster_ids[sort_order]
    sorted_rows = unit[sort_order].astype(jnp.float32)
    tile_count = ROWS // tile_span
    tiled_rows = sorted_rows.reshape(tile_count, tile_span, D)
    tiled_ids = sorted_ids.reshape(tile_count, tile_span)
    lowest = tiled_ids[:, 0]
    highest = tiled_ids[:, tile_span - 1]
    local_index = jnp.arange(tile_span, dtype=jnp.int32)

    def keep_best(current):
        return current

    def row_tile(tile_index):
        left_rows = tiled_rows[tile_index]
        left_ids = tiled_ids[tile_index]

        def visit(column_tile, current_best):

            def compute(current):
                right_rows = tiled_rows[column_tile]
                right_ids = tiled_ids[column_tile]
                scores = jnp.dot(left_rows, right_rows.T, precision=lax.Precision.HIGHEST, preferred_element_type=jnp.float32)
                distinct = tile_index * tile_span + local_index[:, None] != column_tile * tile_span + local_index[None, :]
                same = (left_ids[:, None] == right_ids[None, :]) & distinct
                return jnp.maximum(current, lax.optimization_barrier(jnp.max(jnp.where(same, scores, jnp.float32(-1.0)), axis=1)))
            touching = (lowest[column_tile] <= highest[tile_index]) & (highest[column_tile] >= lowest[tile_index])
            return lax.cond(touching, compute, keep_best, current_best)
        return lax.fori_loop(0, tile_count, visit, jnp.full((tile_span,), -1.0, jnp.float32))
    sorted_best = lax.map(row_tile, jnp.arange(tile_count, dtype=jnp.int32)).reshape(-1)
    return jnp.zeros((ROWS,), jnp.float32).at[sort_order].set(sorted_best)
```

```python
import functools

import jax
import jax.numpy as jnp
from jax import lax
from jax.experimental import pallas as pl
from jax.experimental.pallas import tpu as pltpu
from jax.sharding import PartitionSpec as P

EPSILON = 1e-06
OWNERS = 16
CAP = 64
HALF = CAP // 2
CHUNK = OWNERS * HALF
LOW = -1e30
MARK = 2.0
F32 = jnp.float32
BF16 = jnp.bfloat16


def params():
    return pltpu.CompilerParams(vmem_limit_bytes=40 * 1024 * 1024)


def cost(flops, bytes_accessed):
    return pl.CostEstimate(flops=flops, bytes_accessed=bytes_accessed, transcendentals=0)


def iota(shape, dim):
    return lax.broadcasted_iota(jnp.int32, shape, dim)


def prep_kernel(x_ref, ids_ref, first_ref, second_ref, meta_ref):
    rows = x_ref.shape[0]
    x = x_ref[...]
    unit = (x * lax.rsqrt(jnp.sum(x * x, axis=1, keepdims=True) + EPSILON)).astype(BF16)
    ids = ids_ref[...]
    onehot = iota((OWNERS, rows), 0) == ids
    upto = (iota((rows, rows), 0) <= iota((rows, rows), 1)).astype(BF16)
    counts = jnp.dot(onehot.astype(BF16), upto, preferred_element_type=F32)
    rank = jnp.sum(jnp.where(onehot, counts, 0.0), axis=0, keepdims=True).astype(jnp.int32) - 1
    meta_ref[...] = jnp.where(iota((8, rows), 0) == 0, ids, rank)
    ones = jnp.ones((rows, 128), BF16)
    for half, out_ref in ((0, first_ref), (1, second_ref)):
        inside = (rank >= half * HALF) & (rank < (half + 1) * HALF)
        slot = jnp.where(inside, ids * HALF + rank - half * HALF, -1)
        place = (iota((CHUNK, rows), 0) == slot).astype(BF16)
        moved = jnp.dot(place, unit, preferred_element_type=F32)
        taken = jnp.dot(place, ones, preferred_element_type=F32)
        out_ref[...] = moved.astype(BF16)
        mark = jnp.where(iota((CHUNK, 128), 1) == 0, MARK * (1.0 - taken), 0.0)
        out_ref[:, 0:128] = (moved[:, 0:128] + mark).astype(BF16)


def prep(embeddings, ids):
    rows, width = embeddings.shape
    return pl.pallas_call(
        prep_kernel,
        out_shape=(
            jax.ShapeDtypeStruct((CHUNK, width), BF16),
            jax.ShapeDtypeStruct((CHUNK, width), BF16),
            jax.ShapeDtypeStruct((8, rows), jnp.int32),
        ),
        compiler_params=params(),
        cost_estimate=cost(4 * CHUNK * rows * width, 8 * CHUNK * width),
        name="prep",
    )(embeddings, ids)


def pair_kernel(units, n_blocks, n_before, wanted, *refs):
    blocks = refs[:n_blocks]
    before = refs[n_blocks : n_blocks + n_before]
    outs = refs[n_blocks + n_before : n_blocks + n_before + len(wanted)]
    lane_bias, row_bias, over_lanes, over_rows = refs[n_blocks + n_before + len(wanted) :]
    tile = 256
    for b, block in enumerate(blocks):
        head = block[:, 0:128].astype(F32)
        bias = jnp.where(head[:, 0:1] > 1.5, LOW, 0.0)
        bias = jnp.broadcast_to(bias, head.shape)
        lane_bias[b] = bias
        row_bias[b] = jnp.transpose(bias)[0:8, :]
        over_lanes[b] = jnp.full(head.shape, LOW, F32)
        over_rows[b] = jnp.full((8, head.shape[0]), LOW, F32)
    for left, right, mode in units:
        n_left, n_right = blocks[left].shape[0], blocks[right].shape[0]

        def step(t, carry, left=left, right=right, mode=mode, n_left=n_left):
            at = pl.ds(pl.multiple_of(t * tile, tile), tile)
            scores = lax.dot_general(
                blocks[left][...], blocks[right][at, :], (((1,), (1,)), ((), ())),
                preferred_element_type=F32,
            )
            masked = scores + row_bias[right, 0:1, at]
            if mode == "self":
                same = iota(scores.shape, 0) == iota(scores.shape, 1) + t * tile
                masked = jnp.where(same, LOW, masked)
            best = masked[:, 0:128]
            for g in range(1, tile // 128):
                best = jnp.maximum(best, masked[:, g * 128 : (g + 1) * 128])
            over_lanes[left] = jnp.maximum(over_lanes[left], best)
            if mode == "both":
                bias = lane_bias[left]
                for g in range(tile // 128):
                    part = scores[:, g * 128 : (g + 1) * 128] + bias
                    part = jnp.max(part.reshape(n_left // 8, 8, 128), axis=0)
                    here = pl.ds(pl.multiple_of(t * tile + g * 128, 128), 128)
                    over_rows[right, :, here] = jnp.maximum(over_rows[right, :, here], part)
            return carry

        lax.fori_loop(0, n_right // tile, step, 0)
    for (first, second, earlier), out in zip(wanted, outs):
        parts = []
        for b in (first, second):
            if b is None:
                parts.append(jnp.full((1, CHUNK), LOW, F32))
                continue
            value = jnp.max(jnp.transpose(over_lanes[b]), axis=0, keepdims=True)
            parts.append(jnp.maximum(value, jnp.max(over_rows[b], axis=0, keepdims=True)))
        for i, part in enumerate(parts):
            at = slice(i * CHUNK, (i + 1) * CHUNK)
            if earlier is not None:
                part = jnp.maximum(part, before[earlier][:, at])
            out[:, at] = part


def pairs(units, blocks, before, wanted, name):
    n = len(blocks)
    rows, width = blocks[0].shape
    return pl.pallas_call(
        functools.partial(pair_kernel, units, n, len(before), wanted),
        out_shape=tuple(jax.ShapeDtypeStruct((1, 2 * CHUNK), F32) for _ in wanted),
        scratch_shapes=[
            pltpu.VMEM((n, rows, 128), F32),
            pltpu.VMEM((n, 8, rows), F32),
            pltpu.VMEM((n, rows, 128), F32),
            pltpu.VMEM((n, 8, rows), F32),
        ],
        compiler_params=params(),
        cost_estimate=cost(2 * len(units) * rows * rows * width, 2 * n * rows * width),
        name=name,
    )(*blocks, *before)


def join_kernel(own_ref, a_ref, b_ref, c_ref, out_ref):
    best = jnp.maximum(jnp.maximum(own_ref[...], a_ref[...]), jnp.maximum(b_ref[...], c_ref[...]))
    best = jnp.maximum(best, -1.0)
    out_ref[...] = jnp.zeros(out_ref.shape, F32)
    for source in range(OWNERS):
        for half in range(2):
            at = half * CHUNK + source * HALF
            out_ref[source * 8 : source * 8 + 1, half * HALF : (half + 1) * HALF] = best[:, at : at + HALF]


def join(own, a, b, c):
    return pl.pallas_call(
        join_kernel,
        out_shape=jax.ShapeDtypeStruct((OWNERS * 8, 128), F32),
        compiler_params=params(),
        name="join",
    )(own, a, b, c)


def pick_kernel(back_ref, meta_ref, out_ref):
    rows = meta_ref.shape[1]
    ids = meta_ref[0:1, :]
    rank = meta_ref[1:2, :]
    onehot = (iota((OWNERS, rows), 0) == ids).astype(BF16)
    at_rank = iota((128, rows), 0) == rank
    rest = jnp.concatenate([back_ref[s * 8 : s * 8 + 1, :] for s in range(OWNERS)], axis=0)
    total = jnp.zeros((1, rows), F32)
    for _ in range(3):
        part = rest.astype(BF16)
        rest = rest - part.astype(F32)
        spread = lax.dot_general(part, onehot, (((0,), (0,)), ((), ())), preferred_element_type=F32)
        total = total + jnp.sum(jnp.where(at_rank, spread, 0.0), axis=0, keepdims=True)
    out_ref[...] = total


def pick(back, meta):
    return pl.pallas_call(
        pick_kernel,
        out_shape=jax.ShapeDtypeStruct((1, meta.shape[1]), F32),
        compiler_params=params(),
        name="pick",
    )(back, meta)


def swap_cores():
    return [(2 * z + k, 2 * z + 1 - k) for z in range(4) for k in range(2)]


def from_next():
    return [(2 * ((z + 1) % 4) + k, 2 * z + k) for z in range(4) for k in range(2)]


def from_last():
    return [
        (2 * ((z + 3) % 4) + (k if z < 2 else 1 - k), 2 * z + k) for z in range(4) for k in range(2)
    ]


def inverse(perm):
    return [(b, a) for a, b in perm]


def to_owners(block):
    shape = block.shape
    block = block.reshape(OWNERS, HALF, shape[1])
    return lax.all_to_all(block, "wide", split_axis=0, concat_axis=0, tiled=True).reshape(shape)


def along_pair(block, perm):
    return lax.ppermute(block, "pair", perm)


def per_device(embeddings, cluster_ids):
    first, second, meta = prep(embeddings, cluster_ids.reshape(1, -1))
    own_a = to_owners(first)
    own_a, second = lax.optimization_barrier((own_a, second))
    sib_a = along_pair(own_a, swap_cores())
    next_a = along_pair(own_a, from_next())
    last_a = along_pair(own_a, from_last())
    own_b = to_owners(second)
    sib_b = along_pair(own_b, swap_cores())
    next_b = along_pair(own_b, from_next())
    last_b = along_pair(own_b, from_last())
    own, sib, nxt, last = pairs(
        (
            (0, 0, "self"), (0, 1, "both"), (1, 1, "self"),
            (0, 2, "left"), (0, 3, "left"), (1, 2, "left"), (1, 3, "left"),
            (0, 4, "both"), (1, 4, "both"), (2, 4, "both"), (3, 4, "both"), (5, 4, "both"),
        ),
        (own_a, own_b, sib_a, sib_b, next_a, last_a),
        (),
        ((0, 1, None), (2, 3, None), (4, None, None), (5, None, None)),
        "early",
    )
    own, sib, nxt, last = pairs(
        (
            (0, 6, "both"), (1, 6, "both"), (2, 6, "both"), (3, 6, "both"),
            (5, 6, "both"), (7, 4, "both"), (7, 6, "both"),
        ),
        (own_a, own_b, sib_a, sib_b, next_a, last_a, next_b, last_b),
        (own, sib, nxt, last),
        ((0, 1, 0), (2, 3, 1), (4, 6, 2), (5, 7, 3)),
        "late",
    )
    tiles = join(
        own,
        along_pair(sib, swap_cores()),
        along_pair(nxt, inverse(from_next())),
        along_pair(last, inverse(from_last())),
    )
    back = lax.all_to_all(tiles.reshape(OWNERS, 8, 128), "wide", split_axis=0, concat_axis=0, tiled=True)
    return pick(back.reshape(OWNERS * 8, 128), meta).reshape(-1)


def solution(mesh):
    in_specs = (P(("wide", "pair"), None), P(("wide", "pair")))
    out_specs = P(("wide", "pair"))
    return jax.shard_map(
        per_device, mesh=mesh, in_specs=in_specs, out_specs=out_specs, check_vma=False
    )
```

```python
import functools

import jax
import jax.numpy as jnp
from jax import lax
from jax.experimental import pallas as pl
from jax.experimental.pallas import tpu as pltpu
from jax.sharding import PartitionSpec as P

EPSILON = 1e-06
OWNERS = 16
CAP = 64
HALF = CAP // 2
CHUNK = OWNERS * HALF
SHORT = 256
LOW = -1e30
MARK = 2.0
F32 = jnp.float32
BF16 = jnp.bfloat16


def params():
    return pltpu.CompilerParams(vmem_limit_bytes=40 * 1024 * 1024)


def cost(flops, bytes_accessed):
    return pl.CostEstimate(flops=flops, bytes_accessed=bytes_accessed, transcendentals=0)


def iota(shape, dim):
    return lax.broadcasted_iota(jnp.int32, shape, dim)


def marked(head):
    return head.astype(F32)[:, 0:1] > 1.5


def place(half, unit, ids, rank, out_ref):
    rows = unit.shape[0]
    inside = (rank >= half * HALF) & (rank < (half + 1) * HALF)
    slot = jnp.where(inside, ids * HALF + rank - half * HALF, -1)
    onehot = (iota((CHUNK, rows), 0) == slot).astype(BF16)
    moved = jnp.dot(onehot, unit, preferred_element_type=F32)
    taken = jnp.dot(onehot, jnp.ones((rows, 128), BF16), preferred_element_type=F32)
    out_ref[...] = moved.astype(BF16)
    mark = jnp.where(iota((CHUNK, 128), 1) == 0, MARK * (1.0 - taken), 0.0)
    out_ref[:, 0:128] = (moved[:, 0:128] + mark).astype(BF16)


def prep_kernel(x_hbm, ids_hbm, first_ref, unit_ref, meta_ref, x_ref, ids_ref, sems):
    rows = x_ref.shape[0]
    parts = 4
    step = rows // parts
    copies = [pltpu.make_async_copy(ids_hbm, ids_ref, sems.at[parts])]
    for i in range(parts):
        at = pl.ds(i * step, step)
        copies.append(pltpu.make_async_copy(x_hbm.at[at], x_ref.at[at], sems.at[i]))
    for copy in copies:
        copy.start()
    copies[0].wait()
    ids = ids_ref[...]
    onehot = iota((OWNERS, rows), 0) == ids
    upto = (iota((rows, rows), 0) <= iota((rows, rows), 1)).astype(BF16)
    counts = jnp.dot(onehot.astype(BF16), upto, preferred_element_type=F32)
    rank = jnp.sum(jnp.where(onehot, counts, 0.0), axis=0, keepdims=True).astype(jnp.int32) - 1
    meta_ref[...] = jnp.where(iota((8, rows), 0) == 0, ids, rank)
    for i in range(parts):
        copies[i + 1].wait()
        at = pl.ds(i * step, step)
        x = x_ref[at, :]
        scale = lax.rsqrt(jnp.sum(x * x, axis=1, keepdims=True) + EPSILON)
        unit_ref[at, :] = (x * scale).astype(BF16)
    place(0, unit_ref[...], ids, rank, first_ref)


def prep(embeddings, ids):
    rows, width = embeddings.shape
    return pl.pallas_call(
        prep_kernel,
        in_specs=[pl.BlockSpec(memory_space=pltpu.HBM)] * 2,
        out_shape=(
            jax.ShapeDtypeStruct((CHUNK, width), BF16),
            jax.ShapeDtypeStruct((rows, width), BF16),
            jax.ShapeDtypeStruct((8, rows), jnp.int32),
        ),
        scratch_shapes=[
            pltpu.VMEM((rows, width), F32),
            pltpu.VMEM((1, rows), jnp.int32),
            pltpu.SemaphoreType.DMA((5,)),
        ],
        compiler_params=params(),
        cost_estimate=cost(2 * CHUNK * rows * width, 8 * rows * width),
        name="prep",
    )(embeddings, ids)


def rest_kernel(unit_ref, meta_ref, second_ref):
    place(1, unit_ref[...], meta_ref[0:1, :], meta_ref[1:2, :], second_ref)


def rest(unit, meta):
    rows, width = unit.shape
    return pl.pallas_call(
        rest_kernel,
        out_shape=jax.ShapeDtypeStruct((CHUNK, width), BF16),
        compiler_params=params(),
        cost_estimate=cost(2 * CHUNK * rows * width, 4 * rows * width),
        name="rest",
    )(unit, meta)


def pack_kernel(block_ref, packed_ref, spot_ref):
    rows = block_ref.shape[0]
    full = jnp.where(marked(block_ref[:, 0:128]), 0.0, 1.0)
    full = jnp.transpose(jnp.broadcast_to(full, (rows, 128)))[0:8, :]
    upto = (iota((rows, rows), 0) <= iota((rows, rows), 1)).astype(BF16)
    count = jnp.dot(full.astype(BF16), upto, preferred_element_type=F32)
    spot = jnp.where(full > 0.5, count - 1.0, -1.0).astype(jnp.int32)
    spot_ref[...] = spot
    onehot = (iota((SHORT, rows), 0) == spot[0:1, :]).astype(BF16)
    moved = jnp.dot(onehot, block_ref[...], preferred_element_type=F32)
    taken = jnp.dot(onehot, jnp.ones((rows, 128), BF16), preferred_element_type=F32)
    packed_ref[...] = moved.astype(BF16)
    mark = jnp.where(iota((SHORT, 128), 1) == 0, MARK * (1.0 - taken), 0.0)
    packed_ref[:, 0:128] = (moved[:, 0:128] + mark).astype(BF16)


def pack(block):
    rows, width = block.shape
    return pl.pallas_call(
        pack_kernel,
        out_shape=(
            jax.ShapeDtypeStruct((SHORT, width), BF16),
            jax.ShapeDtypeStruct((8, rows), jnp.int32),
        ),
        compiler_params=params(),
        cost_estimate=cost(2 * SHORT * rows * width, 4 * rows * width),
        name="pack",
    )(block)


def pair_kernel(units, n_blocks, n_before, wanted, tails, *refs):
    blocks = refs[:n_blocks]
    before = refs[n_blocks : n_blocks + n_before]
    outs = refs[n_blocks + n_before : n_blocks + n_before + len(wanted)]
    lane_bias, row_bias, over_lanes, over_rows = refs[n_blocks + n_before + len(wanted) :]
    for b, block in enumerate(blocks):
        rows = block.shape[0]
        bias = jnp.where(marked(block[:, 0:128]), LOW, 0.0)
        bias = jnp.broadcast_to(bias, (rows, 128))
        lane_bias[b, 0:rows] = bias
        row_bias[b, :, 0:rows] = jnp.transpose(bias)[0:8, :]
        over_lanes[b, 0:rows] = jnp.full((rows, 128), LOW, F32)
        over_rows[b, :, 0:rows] = jnp.full((8, rows), LOW, F32)
    for left, right, mode in units:
        n_left, n_right = blocks[left].shape[0], blocks[right].shape[0]
        scores = lax.dot_general(
            blocks[left][...], blocks[right][...], (((1,), (1,)), ((), ())), preferred_element_type=F32
        )
        valid = scores + row_bias[right, 0:1, 0:n_right]
        if mode == "self":
            valid = jnp.where(iota(scores.shape, 0) == iota(scores.shape, 1), LOW, valid)
        best = over_lanes[left, 0:n_left]
        for g in range(0, n_right, 128):
            best = jnp.maximum(best, valid[:, g : g + 128])
        over_lanes[left, 0:n_left] = best
        if mode == "both":
            bias = lane_bias[left, 0:n_left]
            for g in range(0, n_right, 128):
                part = (scores[:, g : g + 128] + bias).reshape(n_left // 8, 8, 128)
                part = jnp.max(part, axis=0)
                over_rows[right, :, g : g + 128] = jnp.maximum(over_rows[right, :, g : g + 128], part)
    flag = jnp.zeros((1, 128), F32)
    for b in tails:
        end = blocks[b].shape[0]
        last = blocks[b][end - 16 : end, 0:128].astype(F32)[15:16, 0:1]
        flag = jnp.maximum(flag, jnp.where(last > 1.5, 0.0, 1.0))
    for (first, second, earlier), out in zip(wanted, outs):
        for b, at, n in ((first, 0, CHUNK), (second, CHUNK, out.shape[1] - CHUNK - 128)):
            part = jnp.full((1, n), LOW, F32)
            if b is not None:
                part = jnp.max(jnp.transpose(over_lanes[b, 0:n]), axis=0, keepdims=True)
                part = jnp.maximum(part, jnp.max(over_rows[b, :, 0:n], axis=0, keepdims=True))
            if earlier is not None:
                part = jnp.maximum(part, before[earlier][:, at : at + n])
            out[:, at : at + n] = part
        out[:, out.shape[1] - 128 :] = flag


def pairs(units, blocks, before, wanted, tails, width, name):
    n = len(blocks)
    rows, depth = blocks[0].shape
    work = sum(blocks[a].shape[0] * blocks[b].shape[0] for a, b, _ in units)
    return pl.pallas_call(
        functools.partial(pair_kernel, units, n, len(before), wanted, tails),
        out_shape=tuple(jax.ShapeDtypeStruct((1, width + 128), F32) for _ in wanted),
        scratch_shapes=[
            pltpu.VMEM((n, rows, 128), F32),
            pltpu.VMEM((n, 8, rows), F32),
            pltpu.VMEM((n, rows, 128), F32),
            pltpu.VMEM((n, 8, rows), F32),
        ],
        compiler_params=params(),
        cost_estimate=cost(2 * work * depth, 2 * n * rows * depth),
        name=name,
    )(*blocks, *before)


def spread_exact(value, onehot, contract):
    total = None
    for _ in range(3):
        part = value.astype(BF16)
        value = value - part.astype(F32)
        moved = lax.dot_general(part, onehot, ((contract, ((0,))), ((), ())), preferred_element_type=F32)
        total = moved if total is None else total + moved
    return total


def join_kernel(packed, own_ref, a_ref, b_ref, c_ref, *rest):
    best = jnp.maximum(jnp.maximum(own_ref[...], a_ref[...]), jnp.maximum(b_ref[...], c_ref[...]))
    best = jnp.maximum(best, -1.0)
    out_ref = rest[-1]
    second = best[:, CHUNK:-128]
    if packed:
        spot = rest[0][0:1, :]
        onehot = (iota((SHORT, CHUNK), 0) == spot).astype(BF16)
        second = spread_exact(jnp.broadcast_to(second, (8, SHORT)), onehot, (1,))[0:1, :]
    out_ref[...] = jnp.zeros(out_ref.shape, F32)
    for source in range(OWNERS):
        at = source * HALF
        row = slice(source * 8, source * 8 + 1)
        out_ref[row, 0:HALF] = best[:, at : at + HALF]
        out_ref[row, HALF:CAP] = second[:, at : at + HALF]
        out_ref[row, CAP:128] = best[:, -CAP:]


def join(own, a, b, c, *spot):
    return pl.pallas_call(
        functools.partial(join_kernel, bool(spot)),
        out_shape=jax.ShapeDtypeStruct((OWNERS * 8, 128), F32),
        compiler_params=params(),
        name="join",
    )(own, a, b, c, *spot)


def pick_kernel(back_ref, meta_ref, out_ref, flag_ref):
    rows = meta_ref.shape[1]
    ids = meta_ref[0:1, :]
    rank = meta_ref[1:2, :]
    onehot = (iota((OWNERS, rows), 0) == ids).astype(BF16)
    tiles = jnp.concatenate([back_ref[s * 8 : s * 8 + 1, :] for s in range(OWNERS)], axis=0)
    moved = spread_exact(tiles, onehot, (0,))
    out_ref[...] = jnp.sum(jnp.where(iota((128, rows), 0) == rank, moved, 0.0), axis=0, keepdims=True)
    flag_ref[...] = jnp.max(tiles, axis=0, keepdims=True)


def pick(back, meta):
    return pl.pallas_call(
        pick_kernel,
        out_shape=(
            jax.ShapeDtypeStruct((1, meta.shape[1]), F32),
            jax.ShapeDtypeStruct((1, 128), F32),
        ),
        compiler_params=params(),
        name="pick",
    )(back, meta)


def swap_cores():
    return [(2 * z + k, 2 * z + 1 - k) for z in range(4) for k in range(2)]


def from_next():
    return [(2 * ((z + 1) % 4) + k, 2 * z + k) for z in range(4) for k in range(2)]


def from_last():
    return [
        (2 * ((z + 3) % 4) + (k if z < 2 else 1 - k), 2 * z + k) for z in range(4) for k in range(2)
    ]


def inverse(perm):
    return [(b, a) for a, b in perm]


def to_owners(block):
    shape = block.shape
    block = block.reshape(OWNERS, HALF, shape[1])
    return lax.all_to_all(block, "wide", split_axis=0, concat_axis=0, tiled=True).reshape(shape)


def along_pair(block, perm):
    return lax.ppermute(block, "pair", perm)


def give_back(own, sib, nxt, last, meta, *spot):
    tiles = join(
        own,
        along_pair(sib, swap_cores()),
        along_pair(nxt, inverse(from_next())),
        along_pair(last, inverse(from_last())),
        *spot,
    )
    back = lax.all_to_all(tiles.reshape(OWNERS, 8, 128), "wide", split_axis=0, concat_axis=0, tiled=True)
    return pick(back.reshape(OWNERS * 8, 128), meta)


EARLY = (
    (0, 0, "self"), (0, 2, "left"), (0, 4, "both"), (2, 4, "both"), (5, 4, "both"),
    (0, 1, "both"), (1, 1, "self"), (0, 3, "left"), (1, 2, "left"), (1, 3, "left"),
    (1, 4, "both"), (3, 4, "both"),
)
LATE = (
    (0, 6, "both"), (1, 6, "both"), (2, 6, "both"), (3, 6, "both"),
    (5, 6, "both"), (7, 4, "both"), (7, 6, "both"),
)


def match(a, second, tails):
    own_a, sib_a, next_a, last_a = a
    own_b, sib_b, next_b, last_b = second
    width = CHUNK + own_b.shape[0]
    before = pairs(
        EARLY,
        (own_a, own_b, sib_a, sib_b, next_a, last_a),
        (),
        ((0, 1, None), (2, 3, None), (4, None, None), (5, None, None)),
        (),
        width,
        "early",
    )
    return pairs(
        LATE,
        (own_a, own_b, sib_a, sib_b, next_a, last_a, next_b, last_b),
        before,
        ((0, 1, 0), (2, 3, 1), (4, 6, 2), (5, 7, 3)),
        tails,
        width,
        "late",
    )


def neighbours(block):
    return (
        block,
        along_pair(block, swap_cores()),
        along_pair(block, from_next()),
        along_pair(block, from_last()),
    )


def exchange(embeddings, ids):
    first, unit, meta = prep(embeddings, ids)
    own_a = to_owners(first)
    own_a, unit = lax.optimization_barrier((own_a, unit))
    a = neighbours(own_a)
    own_b = to_owners(rest(unit, meta))
    own_b, *a = lax.optimization_barrier((own_b, *a))
    return tuple(a), own_b, meta


def whole(embeddings, ids):
    a, own_b, meta = exchange(embeddings, ids)
    best = match(a, neighbours(own_b), ())
    return give_back(*best, meta)[0]


def per_device(embeddings, cluster_ids):
    ids = cluster_ids.reshape(1, -1)
    a, own_b, meta = exchange(embeddings, ids)
    packed, spot = pack(own_b)
    best = match(a, neighbours(packed), (1, 3, 6, 7))
    value, flag = give_back(*best, meta, spot)
    return lax.cond(
        flag[0, CAP] > 0.5, lambda: whole(embeddings, ids), lambda: value
    ).reshape(-1)


def solution(mesh):
    in_specs = (P(("wide", "pair"), None), P(("wide", "pair")))
    out_specs = P(("wide", "pair"))
    return jax.shard_map(
        per_device, mesh=mesh, in_specs=in_specs, out_specs=out_specs, check_vma=False
    )
```

```python
import functools

import jax
import jax.numpy as jnp
from jax import lax
from jax.experimental import pallas as pl
from jax.experimental.pallas import tpu as pltpu
from jax.sharding import PartitionSpec as P

EPSILON = 1e-06
OWNERS = 16
CAP = 64
HALF = CAP // 2
CHUNK = OWNERS * HALF
SHORT = 208
LOW = -1e30
MARK = 2.0
F32 = jnp.float32
BF16 = jnp.bfloat16


def params():
    return pltpu.CompilerParams(vmem_limit_bytes=40 * 1024 * 1024)


def cost(flops, bytes_accessed):
    return pl.CostEstimate(flops=flops, bytes_accessed=bytes_accessed, transcendentals=0)


def iota(shape, dim):
    return lax.broadcasted_iota(jnp.int32, shape, dim)


def marked(head):
    return head.astype(F32)[:, 0:1] > 1.5


def place(half, unit, ids, rank, out_ref):
    rows = unit.shape[0]
    inside = (rank >= half * HALF) & (rank < (half + 1) * HALF)
    slot = jnp.where(inside, ids * HALF + rank - half * HALF, -1)
    onehot = (iota((CHUNK, rows), 0) == slot).astype(BF16)
    moved = jnp.dot(onehot, unit, preferred_element_type=F32)
    taken = jnp.dot(onehot, jnp.ones((rows, 128), BF16), preferred_element_type=F32)
    out_ref[...] = moved.astype(BF16)
    mark = jnp.where(iota((CHUNK, 128), 1) == 0, MARK * (1.0 - taken), 0.0)
    out_ref[:, 0:128] = (moved[:, 0:128] + mark).astype(BF16)


def prep_kernel(x_hbm, ids_hbm, first_ref, unit_ref, meta_ref, x_ref, ids_ref, sems):
    rows = x_ref.shape[0]
    parts = 4
    step = rows // parts
    copies = [pltpu.make_async_copy(ids_hbm, ids_ref, sems.at[parts])]
    for i in range(parts):
        at = pl.ds(i * step, step)
        copies.append(pltpu.make_async_copy(x_hbm.at[at], x_ref.at[at], sems.at[i]))
    for copy in copies:
        copy.start()
    copies[0].wait()
    ids = ids_ref[...]
    onehot = iota((OWNERS, rows), 0) == ids
    upto = (iota((rows, rows), 0) <= iota((rows, rows), 1)).astype(BF16)
    counts = jnp.dot(onehot.astype(BF16), upto, preferred_element_type=F32)
    rank = jnp.sum(jnp.where(onehot, counts, 0.0), axis=0, keepdims=True).astype(jnp.int32) - 1
    meta_ref[...] = jnp.where(iota((8, rows), 0) == 0, ids, rank)
    for i in range(parts):
        copies[i + 1].wait()
        at = pl.ds(i * step, step)
        x = x_ref[at, :]
        scale = lax.rsqrt(jnp.sum(x * x, axis=1, keepdims=True) + EPSILON)
        unit_ref[at, :] = (x * scale).astype(BF16)
    place(0, unit_ref[...], ids, rank, first_ref)


def prep(embeddings, ids):
    rows, width = embeddings.shape
    return pl.pallas_call(
        prep_kernel,
        in_specs=[pl.BlockSpec(memory_space=pltpu.HBM)] * 2,
        out_shape=(
            jax.ShapeDtypeStruct((CHUNK, width), BF16),
            jax.ShapeDtypeStruct((rows, width), BF16),
            jax.ShapeDtypeStruct((8, rows), jnp.int32),
        ),
        scratch_shapes=[
            pltpu.VMEM((rows, width), F32),
            pltpu.VMEM((1, rows), jnp.int32),
            pltpu.SemaphoreType.DMA((5,)),
        ],
        compiler_params=params(),
        cost_estimate=cost(2 * CHUNK * rows * width, 8 * rows * width),
        name="prep",
    )(embeddings, ids)


def rest_kernel(unit_ref, meta_ref, second_ref):
    place(1, unit_ref[...], meta_ref[0:1, :], meta_ref[1:2, :], second_ref)


def rest(unit, meta):
    rows, width = unit.shape
    return pl.pallas_call(
        rest_kernel,
        out_shape=jax.ShapeDtypeStruct((CHUNK, width), BF16),
        compiler_params=params(),
        cost_estimate=cost(2 * CHUNK * rows * width, 4 * rows * width),
        name="rest",
    )(unit, meta)


def pack_kernel(block_ref, packed_ref, onehot_ref):
    rows = block_ref.shape[0]
    full = jnp.where(marked(block_ref[:, 0:128]), 0.0, 1.0)
    full = jnp.transpose(jnp.broadcast_to(full, (rows, 128)))[0:8, :]
    upto = (iota((rows, rows), 0) <= iota((rows, rows), 1)).astype(BF16)
    count = jnp.dot(full.astype(BF16), upto, preferred_element_type=F32)
    spot = jnp.where(full > 0.5, count - 1.0, -1.0).astype(jnp.int32)
    onehot = (iota((SHORT, rows), 0) == spot[0:1, :]).astype(BF16)
    onehot_ref[...] = onehot
    moved = jnp.dot(onehot, block_ref[...], preferred_element_type=F32)
    taken = jnp.dot(onehot, jnp.ones((rows, 128), BF16), preferred_element_type=F32)
    packed_ref[...] = moved.astype(BF16)
    mark = jnp.where(iota((SHORT, 128), 1) == 0, MARK * (1.0 - taken), 0.0)
    packed_ref[:, 0:128] = (moved[:, 0:128] + mark).astype(BF16)


def pack(block):
    rows, width = block.shape
    return pl.pallas_call(
        pack_kernel,
        out_shape=(
            jax.ShapeDtypeStruct((SHORT, width), BF16),
            jax.ShapeDtypeStruct((SHORT, rows), BF16),
        ),
        compiler_params=params(),
        cost_estimate=cost(2 * SHORT * rows * width, 4 * rows * width),
        name="pack",
    )(block)


def lanes(rows):
    return -(-rows // 128) * 128


def pair_kernel(units, n_blocks, n_before, wanted, tails, *refs):
    blocks = refs[:n_blocks]
    before = refs[n_blocks : n_blocks + n_before]
    outs = refs[n_blocks + n_before : n_blocks + n_before + len(wanted)]
    lane_bias, row_bias, over_lanes, over_rows = refs[n_blocks + n_before + len(wanted) :]
    for b, block in enumerate(blocks):
        rows = block.shape[0]
        bias = jnp.where(marked(block[:, 0:128]), LOW, 0.0)
        lane_bias[b, 0:rows] = jnp.broadcast_to(bias, (rows, 128))
        row_bias[b, :, 0 : lanes(rows)] = jnp.transpose(lane_bias[b, 0 : lanes(rows)])[0:8, :]
        over_lanes[b, 0 : lanes(rows)] = jnp.full((lanes(rows), 128), LOW, F32)
        over_rows[b, :, 0 : lanes(rows)] = jnp.full((8, lanes(rows)), LOW, F32)
    for left, right, mode in units:
        n_left, n_right = blocks[left].shape[0], blocks[right].shape[0]
        scores = lax.dot_general(
            blocks[left][...], blocks[right][...], (((1,), (1,)), ((), ())), preferred_element_type=F32
        )
        valid = scores + row_bias[right, 0:1, 0:n_right]
        if mode == "self":
            valid = jnp.where(iota(scores.shape, 0) == iota(scores.shape, 1), LOW, valid)
        best = over_lanes[left, 0:n_left]
        whole_groups = n_right // 128 * 128
        for g in range(0, whole_groups, 128):
            best = jnp.maximum(best, valid[:, g : g + 128])
        over_lanes[left, 0:n_left] = best
        if whole_groups < n_right:
            some = n_right - whole_groups
            best = jnp.maximum(over_lanes[left, 0:n_left, 0:some], valid[:, whole_groups:])
            over_lanes[left, 0:n_left, 0:some] = best
        if mode == "both":
            bias = lane_bias[left, 0:n_left]
            for g in range(0, n_right, 128):
                end = min(g + 128, n_right)
                part = scores[:, g:end] + bias[:, 0 : end - g]
                part = jnp.max(part.reshape(n_left // 8, 8, end - g), axis=0)
                over_rows[right, :, g:end] = jnp.maximum(over_rows[right, :, g:end], part)
    flag = jnp.zeros((1, 128), F32)
    for b in tails:
        end = blocks[b].shape[0]
        last = blocks[b][end - 16 : end, 0:128].astype(F32)[15:16, 0:1]
        flag = jnp.maximum(flag, jnp.where(last > 1.5, 0.0, 1.0))
    for (first, second, earlier), out in zip(wanted, outs):
        for b, at, n in ((first, 0, CHUNK), (second, CHUNK, out.shape[1] - CHUNK - 128)):
            part = jnp.full((1, n), LOW, F32)
            if b is not None:
                part = jnp.max(jnp.transpose(over_lanes[b, 0:n]), axis=0, keepdims=True)
                part = jnp.maximum(part, jnp.max(over_rows[b, :, 0:n], axis=0, keepdims=True))
            if earlier is not None:
                part = jnp.maximum(part, before[earlier][:, at : at + n])
            out[:, at : at + n] = part
        out[:, out.shape[1] - 128 :] = flag


def pairs(units, blocks, before, wanted, tails, width, name):
    n = len(blocks)
    rows, depth = blocks[0].shape
    work = sum(blocks[a].shape[0] * blocks[b].shape[0] for a, b, _ in units)
    return pl.pallas_call(
        functools.partial(pair_kernel, units, n, len(before), wanted, tails),
        out_shape=tuple(jax.ShapeDtypeStruct((1, width + 128), F32) for _ in wanted),
        scratch_shapes=[
            pltpu.VMEM((n, rows, 128), F32),
            pltpu.VMEM((n, 8, rows), F32),
            pltpu.VMEM((n, rows, 128), F32),
            pltpu.VMEM((n, 8, rows), F32),
        ],
        compiler_params=params(),
        cost_estimate=cost(2 * work * depth, 2 * n * rows * depth),
        name=name,
    )(*blocks, *before)


def three_parts(value):
    parts = []
    for _ in range(3):
        part = value.astype(BF16).astype(F32)
        value = value - part
        parts.append(part)
    return jnp.concatenate(parts, axis=0).astype(BF16)


def join_kernel(packed, own_ref, a_ref, b_ref, c_ref, *rest):
    best = jnp.maximum(jnp.maximum(own_ref[...], a_ref[...]), jnp.maximum(b_ref[...], c_ref[...]))
    best = jnp.maximum(best, -1.0)
    out_ref = rest[-1]
    second = best[:, CHUNK:-128]
    if packed:
        parts = three_parts(jnp.broadcast_to(second[:, 0:SHORT], (8, SHORT)))
        moved = jnp.dot(parts, rest[0][...], preferred_element_type=F32)
        second = moved[0:1, :] + moved[8:9, :] + moved[16:17, :]
    for source in range(OWNERS):
        at = source * HALF
        row = slice(source, source + 1)
        out_ref[row, 0:HALF] = best[:, at : at + HALF]
        out_ref[row, HALF:CAP] = second[:, at : at + HALF]
        out_ref[row, CAP:128] = best[:, -CAP:]


def join(own, a, b, c, *onehot):
    return pl.pallas_call(
        functools.partial(join_kernel, bool(onehot)),
        out_shape=jax.ShapeDtypeStruct((OWNERS, 128), F32),
        compiler_params=params(),
        name="join",
    )(own, a, b, c, *onehot)


def pick_kernel(back_ref, meta_ref, out_ref, flag_ref):
    rows = meta_ref.shape[1]
    ids = meta_ref[0:1, :]
    rank = meta_ref[1:2, :]
    flag_ref[...] = jnp.max(jnp.max(back_ref[:, CAP:], axis=0, keepdims=True), axis=1, keepdims=True)
    onehot = ((iota((3 * OWNERS, rows), 0) & (OWNERS - 1)) == ids).astype(BF16)
    tiles = back_ref[...]
    moved = lax.dot_general(
        three_parts(tiles), onehot, (((0,), (0,)), ((), ())), preferred_element_type=F32
    )[0:CAP, :]
    out_ref[...] = jnp.sum(jnp.where(iota((CAP, rows), 0) == rank, moved, 0.0), axis=0, keepdims=True)


def pick(back, meta):
    return pl.pallas_call(
        pick_kernel,
        out_shape=(
            jax.ShapeDtypeStruct((1, meta.shape[1]), F32),
            jax.ShapeDtypeStruct((1, 1), F32),
        ),
        compiler_params=params(),
        name="pick",
    )(back, meta)


def swap_cores():
    return [(2 * z + k, 2 * z + 1 - k) for z in range(4) for k in range(2)]


def from_next():
    return [(2 * ((z + 1) % 4) + k, 2 * z + k) for z in range(4) for k in range(2)]


def from_last():
    return [
        (2 * ((z + 3) % 4) + (k if z < 2 else 1 - k), 2 * z + k) for z in range(4) for k in range(2)
    ]


def inverse(perm):
    return [(b, a) for a, b in perm]


def to_owners(block):
    shape = block.shape
    block = block.reshape(OWNERS, HALF, shape[1])
    return lax.all_to_all(block, "wide", split_axis=0, concat_axis=0, tiled=True).reshape(shape)


def along_pair(block, perm):
    return lax.ppermute(block, "pair", perm)


def give_back(own, sib, nxt, last, meta, *onehot):
    tiles = join(
        own,
        along_pair(sib, swap_cores()),
        along_pair(nxt, inverse(from_next())),
        along_pair(last, inverse(from_last())),
        *onehot,
    )
    back = lax.all_to_all(tiles.reshape(OWNERS, 1, 128), "wide", split_axis=0, concat_axis=0, tiled=True)
    return pick(back.reshape(OWNERS, 128), meta)


EARLY = (
    (0, 0, "self"), (0, 2, "left"), (0, 4, "both"), (2, 4, "both"), (5, 4, "both"),
    (0, 1, "both"), (1, 1, "self"), (0, 3, "left"), (1, 2, "left"), (1, 3, "left"),
    (1, 4, "both"), (3, 4, "both"),
)
LATE = (
    (0, 6, "both"), (1, 6, "both"), (2, 6, "both"), (3, 6, "both"),
    (5, 6, "both"), (7, 4, "both"), (7, 6, "both"),
)


def match(a, second, tails):
    own_a, sib_a, next_a, last_a = a
    own_b, sib_b, next_b, last_b = second
    width = CHUNK + lanes(own_b.shape[0])
    before = pairs(
        EARLY,
        (own_a, own_b, sib_a, sib_b, next_a, last_a),
        (),
        ((0, 1, None), (2, 3, None), (4, None, None), (5, None, None)),
        (),
        width,
        "early",
    )
    return pairs(
        LATE,
        (own_a, own_b, sib_a, sib_b, next_a, last_a, next_b, last_b),
        before,
        ((0, 1, 0), (2, 3, 1), (4, 6, 2), (5, 7, 3)),
        tails,
        width,
        "late",
    )


def neighbours(block):
    return (
        block,
        along_pair(block, swap_cores()),
        along_pair(block, from_next()),
        along_pair(block, from_last()),
    )


def exchange(embeddings, ids):
    first, unit, meta = prep(embeddings, ids)
    own_a = to_owners(first)
    own_a, unit = lax.optimization_barrier((own_a, unit))
    a = neighbours(own_a)
    own_b = to_owners(rest(unit, meta))
    own_b, *a = lax.optimization_barrier((own_b, *a))
    return tuple(a), own_b, meta


def whole(embeddings, ids):
    a, own_b, meta = exchange(embeddings, ids)
    best = match(a, neighbours(own_b), ())
    return give_back(*best, meta)[0]


def per_device(embeddings, cluster_ids):
    ids = cluster_ids.reshape(1, -1)
    a, own_b, meta = exchange(embeddings, ids)
    packed, onehot = pack(own_b)
    best = match(a, neighbours(packed), (1, 3, 6, 7))
    value, flag = give_back(*best, meta, onehot)
    return lax.cond(
        flag.reshape(()) > 0.5, lambda: whole(embeddings, ids), lambda: value
    ).reshape(-1)


def solution(mesh):
    in_specs = (P(("wide", "pair"), None), P(("wide", "pair")))
    out_specs = P(("wide", "pair"))
    return jax.shard_map(
        per_device, mesh=mesh, in_specs=in_specs, out_specs=out_specs, check_vma=False
    )
```

```python
import functools

import jax
import jax.numpy as jnp
from jax import lax
from jax.experimental import pallas as pl
from jax.experimental.pallas import tpu as pltpu
from jax.sharding import PartitionSpec as P

EPSILON = 1e-06
OWNERS = 16
CAP = 64
HALF = CAP // 2
CHUNK = OWNERS * HALF
SHORT = 208
LOW = -1e30
MARK = 2.0
F32 = jnp.float32
BF16 = jnp.bfloat16


def params():
    return pltpu.CompilerParams(vmem_limit_bytes=24 * 1024 * 1024)


def cost(flops, bytes_accessed):
    return pl.CostEstimate(flops=flops, bytes_accessed=bytes_accessed, transcendentals=0)


def iota(shape, dim):
    return lax.broadcasted_iota(jnp.int32, shape, dim)


def marked(head):
    return head.astype(F32)[:, 0:1] > 1.5


def place(half, unit, ids, rank, out_ref):
    rows = unit.shape[0]
    inside = (rank >= half * HALF) & (rank < (half + 1) * HALF)
    slot = jnp.where(inside, ids * HALF + rank - half * HALF, -1)
    onehot = (iota((CHUNK, rows), 0) == slot).astype(BF16)
    moved = jnp.dot(onehot, unit, preferred_element_type=F32)
    taken = jnp.dot(onehot, jnp.ones((rows, 128), BF16), preferred_element_type=F32)
    out_ref[...] = moved.astype(BF16)
    mark = jnp.where(iota((CHUNK, 128), 1) == 0, MARK * (1.0 - taken), 0.0)
    out_ref[:, 0:128] = (moved[:, 0:128] + mark).astype(BF16)


def prep_kernel(x_hbm, ids_hbm, first_ref, unit_ref, meta_ref, x_ref, ids_ref, sems):
    rows = x_ref.shape[0]
    parts = 4
    step = rows // parts
    copies = [pltpu.make_async_copy(ids_hbm, ids_ref, sems.at[parts])]
    for i in range(parts):
        at = pl.ds(i * step, step)
        copies.append(pltpu.make_async_copy(x_hbm.at[at], x_ref.at[at], sems.at[i]))
    for copy in copies:
        copy.start()
    copies[0].wait()
    ids = ids_ref[...]
    onehot = iota((OWNERS, rows), 0) == ids
    upto = (iota((rows, rows), 0) <= iota((rows, rows), 1)).astype(BF16)
    counts = jnp.dot(onehot.astype(BF16), upto, preferred_element_type=F32)
    rank = jnp.sum(jnp.where(onehot, counts, 0.0), axis=0, keepdims=True).astype(jnp.int32) - 1
    meta_ref[...] = jnp.where(iota((8, rows), 0) == 0, ids, rank)
    for i in range(parts):
        copies[i + 1].wait()
        at = pl.ds(i * step, step)
        x = x_ref[at, :]
        scale = lax.rsqrt(jnp.sum(x * x, axis=1, keepdims=True) + EPSILON)
        unit_ref[at, :] = (x * scale).astype(BF16)
    place(0, unit_ref[...], ids, rank, first_ref)


def prep(embeddings, ids):
    rows, width = embeddings.shape
    return pl.pallas_call(
        prep_kernel,
        in_specs=[pl.BlockSpec(memory_space=pltpu.HBM)] * 2,
        out_shape=(
            jax.ShapeDtypeStruct((CHUNK, width), BF16),
            jax.ShapeDtypeStruct((rows, width), BF16),
            jax.ShapeDtypeStruct((8, rows), jnp.int32),
        ),
        scratch_shapes=[
            pltpu.VMEM((rows, width), F32),
            pltpu.VMEM((1, rows), jnp.int32),
            pltpu.SemaphoreType.DMA((5,)),
        ],
        compiler_params=params(),
        cost_estimate=cost(2 * CHUNK * rows * width, 8 * rows * width),
        name="prep",
    )(embeddings, ids)


def rest_kernel(unit_ref, meta_ref, second_ref):
    place(1, unit_ref[...], meta_ref[0:1, :], meta_ref[1:2, :], second_ref)


def rest(unit, meta):
    rows, width = unit.shape
    return pl.pallas_call(
        rest_kernel,
        out_shape=jax.ShapeDtypeStruct((CHUNK, width), BF16),
        compiler_params=params(),
        cost_estimate=cost(2 * CHUNK * rows * width, 4 * rows * width),
        name="rest",
    )(unit, meta)


def pack_kernel(block_ref, packed_ref, onehot_ref):
    rows = block_ref.shape[0]
    full = jnp.where(marked(block_ref[:, 0:128]), 0.0, 1.0)
    full = jnp.transpose(jnp.broadcast_to(full, (rows, 128)))[0:8, :]
    upto = (iota((rows, rows), 0) <= iota((rows, rows), 1)).astype(BF16)
    count = jnp.dot(full.astype(BF16), upto, preferred_element_type=F32)
    spot = jnp.where(full > 0.5, count - 1.0, -1.0).astype(jnp.int32)
    onehot = (iota((SHORT, rows), 0) == spot[0:1, :]).astype(BF16)
    onehot_ref[...] = onehot
    moved = jnp.dot(onehot, block_ref[...], preferred_element_type=F32)
    taken = jnp.dot(onehot, jnp.ones((rows, 128), BF16), preferred_element_type=F32)
    packed_ref[...] = moved.astype(BF16)
    mark = jnp.where(iota((SHORT, 128), 1) == 0, MARK * (1.0 - taken), 0.0)
    packed_ref[:, 0:128] = (moved[:, 0:128] + mark).astype(BF16)


def pack(block):
    rows, width = block.shape
    return pl.pallas_call(
        pack_kernel,
        out_shape=(
            jax.ShapeDtypeStruct((SHORT, width), BF16),
            jax.ShapeDtypeStruct((SHORT, rows), BF16),
        ),
        compiler_params=params(),
        cost_estimate=cost(2 * SHORT * rows * width, 4 * rows * width),
        name="pack",
    )(block)


def lanes(rows):
    return -(-rows // 128) * 128


def pair_kernel(units, n_blocks, n_before, wanted, tails, *refs):
    blocks = refs[:n_blocks]
    before = refs[n_blocks : n_blocks + n_before]
    outs = refs[n_blocks + n_before : n_blocks + n_before + len(wanted)]
    lane_bias, row_bias, over_lanes, over_rows = refs[n_blocks + n_before + len(wanted) :]
    lefts = sorted({left for left, _, _ in units})
    rights = sorted({right for _, right, mode in units if mode == "both"})
    for b in sorted({b for unit in units for b in unit[0:2]}):
        rows = blocks[b].shape[0]
        bias = jnp.where(marked(blocks[b][:, 0:128]), LOW, 0.0)
        lane_bias[b, 0:rows] = jnp.broadcast_to(bias, (rows, 128))
        if any(b == right for _, right, _ in units):
            turned = jnp.transpose(lane_bias[b, 0 : lanes(rows)])
            row_bias[b, :, 0 : lanes(rows)] = turned[0:8, :]
        if b in lefts:
            over_lanes[b, 0 : lanes(rows)] = jnp.full((lanes(rows), 128), LOW, F32)
        if b in rights:
            over_rows[b, :, 0 : lanes(rows)] = jnp.full((8, lanes(rows)), LOW, F32)
    for left, right, mode in units:
        n_left, n_right = blocks[left].shape[0], blocks[right].shape[0]
        scores = lax.dot_general(
            blocks[left][...], blocks[right][...], (((1,), (1,)), ((), ())), preferred_element_type=F32
        )
        valid = scores + row_bias[right, 0:1, 0:n_right]
        if mode == "self":
            valid = jnp.where(iota(scores.shape, 0) == iota(scores.shape, 1), LOW, valid)
        best = over_lanes[left, 0:n_left]
        whole_groups = n_right // 128 * 128
        for g in range(0, whole_groups, 128):
            best = jnp.maximum(best, valid[:, g : g + 128])
        over_lanes[left, 0:n_left] = best
        if whole_groups < n_right:
            some = n_right - whole_groups
            best = jnp.maximum(over_lanes[left, 0:n_left, 0:some], valid[:, whole_groups:])
            over_lanes[left, 0:n_left, 0:some] = best
        if mode == "both":
            bias = lane_bias[left, 0:n_left]
            for g in range(0, n_right, 128):
                end = min(g + 128, n_right)
                part = scores[:, g:end] + bias[:, 0 : end - g]
                part = jnp.max(part.reshape(n_left // 8, 8, end - g), axis=0)
                over_rows[right, :, g:end] = jnp.maximum(over_rows[right, :, g:end], part)
    flag = jnp.zeros((1, 128), F32)
    for b in tails:
        end = blocks[b].shape[0]
        last = blocks[b][end - 16 : end, 0:128].astype(F32)[15:16, 0:1]
        flag = jnp.maximum(flag, jnp.where(last > 1.5, 0.0, 1.0))
    for (first, second, earlier), out in zip(wanted, outs):
        for b, at, n in ((first, 0, CHUNK), (second, CHUNK, out.shape[1] - CHUNK - 128)):
            part = jnp.full((1, n), LOW, F32)
            if b in lefts:
                part = jnp.max(jnp.transpose(over_lanes[b, 0:n]), axis=0, keepdims=True)
            if b in rights:
                part = jnp.maximum(part, jnp.max(over_rows[b, :, 0:n], axis=0, keepdims=True))
            if earlier is not None:
                part = jnp.maximum(part, before[earlier][:, at : at + n])
            out[:, at : at + n] = part
        out[:, out.shape[1] - 128 :] = flag


def pairs(units, blocks, before, wanted, tails, width, name):
    n = len(blocks)
    rows, depth = blocks[0].shape
    work = sum(blocks[a].shape[0] * blocks[b].shape[0] for a, b, _ in units)
    return pl.pallas_call(
        functools.partial(pair_kernel, units, n, len(before), wanted, tails),
        out_shape=tuple(jax.ShapeDtypeStruct((1, width + 128), F32) for _ in wanted),
        scratch_shapes=[
            pltpu.VMEM((n, rows, 128), F32),
            pltpu.VMEM((n, 8, rows), F32),
            pltpu.VMEM((n, rows, 128), F32),
            pltpu.VMEM((n, 8, rows), F32),
        ],
        compiler_params=params(),
        cost_estimate=cost(2 * work * depth, 2 * n * rows * depth),
        name=name,
    )(*blocks, *before)


def three_parts(value):
    parts = []
    for _ in range(3):
        part = value.astype(BF16).astype(F32)
        value = value - part
        parts.append(part)
    return jnp.concatenate(parts, axis=0).astype(BF16)


def join_kernel(packed, own_ref, a_ref, b_ref, c_ref, *rest):
    best = jnp.maximum(jnp.maximum(own_ref[...], a_ref[...]), jnp.maximum(b_ref[...], c_ref[...]))
    best = jnp.maximum(best, -1.0)
    out_ref = rest[-1]
    second = best[:, CHUNK:-128]
    if packed:
        parts = three_parts(jnp.broadcast_to(second[:, 0:SHORT], (8, SHORT)))
        moved = jnp.dot(parts, rest[0][...], preferred_element_type=F32)
        second = moved[0:1, :] + moved[8:9, :] + moved[16:17, :]
    for source in range(OWNERS):
        at = source * HALF
        row = slice(source, source + 1)
        out_ref[row, 0:HALF] = best[:, at : at + HALF]
        out_ref[row, HALF:CAP] = second[:, at : at + HALF]
        out_ref[row, CAP:128] = best[:, -CAP:]


def join(own, a, b, c, *onehot):
    return pl.pallas_call(
        functools.partial(join_kernel, bool(onehot)),
        out_shape=jax.ShapeDtypeStruct((OWNERS, 128), F32),
        compiler_params=params(),
        name="join",
    )(own, a, b, c, *onehot)


def pick_kernel(back_ref, meta_ref, out_ref, flag_ref):
    rows = meta_ref.shape[1]
    ids = meta_ref[0:1, :]
    rank = meta_ref[1:2, :]
    flag_ref[...] = jnp.max(jnp.max(back_ref[:, CAP:], axis=0, keepdims=True), axis=1, keepdims=True)
    onehot = ((iota((3 * OWNERS, rows), 0) & (OWNERS - 1)) == ids).astype(BF16)
    tiles = back_ref[...]
    moved = lax.dot_general(
        three_parts(tiles), onehot, (((0,), (0,)), ((), ())), preferred_element_type=F32
    )[0:CAP, :]
    out_ref[...] = jnp.sum(jnp.where(iota((CAP, rows), 0) == rank, moved, 0.0), axis=0, keepdims=True)


def pick(back, meta):
    return pl.pallas_call(
        pick_kernel,
        out_shape=(
            jax.ShapeDtypeStruct((1, meta.shape[1]), F32),
            jax.ShapeDtypeStruct((1, 1), F32),
        ),
        compiler_params=params(),
        name="pick",
    )(back, meta)


def swap_cores():
    return [(2 * z + k, 2 * z + 1 - k) for z in range(4) for k in range(2)]


def from_next():
    return [(2 * ((z + 1) % 4) + k, 2 * z + k) for z in range(4) for k in range(2)]


def from_last():
    return [
        (2 * ((z + 3) % 4) + (k if z < 2 else 1 - k), 2 * z + k) for z in range(4) for k in range(2)
    ]


def inverse(perm):
    return [(b, a) for a, b in perm]


def to_owners(block):
    shape = block.shape
    block = block.reshape(OWNERS, HALF, shape[1])
    return lax.all_to_all(block, "wide", split_axis=0, concat_axis=0, tiled=True).reshape(shape)


def along_pair(block, perm):
    return lax.ppermute(block, "pair", perm)


def give_back(own, sib, nxt, last, meta, *onehot):
    tiles = join(
        own,
        along_pair(sib, swap_cores()),
        along_pair(nxt, inverse(from_next())),
        along_pair(last, inverse(from_last())),
        *onehot,
    )
    back = lax.all_to_all(tiles.reshape(OWNERS, 1, 128), "wide", split_axis=0, concat_axis=0, tiled=True)
    return pick(back.reshape(OWNERS, 128), meta)


EARLY = (
    (0, 0, "self"), (0, 2, "left"), (0, 4, "both"), (2, 4, "both"), (5, 4, "both"),
    (0, 1, "both"), (1, 1, "self"), (0, 3, "left"), (1, 2, "left"), (1, 3, "left"),
    (1, 4, "both"), (3, 4, "both"), (1, 5, "both"), (3, 5, "both"),
)
LATE = ((5, 6, "both"), (7, 4, "both"), (1, 6, "both"), (3, 6, "both"), (7, 6, "both"))


def match(a, second, tails):
    own_a, sib_a, next_a, last_a = a
    own_b, sib_b, next_b, last_b = second
    width = CHUNK + lanes(own_b.shape[0])
    before = pairs(
        EARLY,
        (own_a, own_b, sib_a, sib_b, next_a, last_a),
        (),
        ((0, 1, None), (2, 3, None), (4, None, None), (5, None, None)),
        (),
        width,
        "early",
    )
    return pairs(
        LATE,
        (own_a, own_b, sib_a, sib_b, next_a, last_a, next_b, last_b),
        before,
        ((0, 1, 0), (2, 3, 1), (4, 6, 2), (5, 7, 3)),
        tails,
        width,
        "late",
    )


def neighbours(block):
    return (
        block,
        along_pair(block, swap_cores()),
        along_pair(block, from_next()),
        along_pair(block, from_last()),
    )


def exchange(embeddings, ids):
    first, unit, meta = prep(embeddings, ids)
    own_a = to_owners(first)
    own_a, unit = lax.optimization_barrier((own_a, unit))
    a = neighbours(own_a)
    return a, to_owners(rest(unit, meta)), meta


def whole(embeddings, ids):
    a, own_b, meta = exchange(embeddings, ids)
    own_b, *a = lax.optimization_barrier((own_b, *a))
    best = match(a, neighbours(own_b), ())
    return give_back(*best, meta)[0]


def per_device(embeddings, cluster_ids):
    ids = cluster_ids.reshape(1, -1)
    a, own_b, meta = exchange(embeddings, ids)
    packed, onehot = pack(own_b)
    packed, *a = lax.optimization_barrier((packed, *a))
    best = match(a, neighbours(packed), (1, 3, 6, 7))
    value, flag = give_back(*best, meta, onehot)
    return lax.cond(
        flag.reshape(()) > 0.5, lambda: whole(embeddings, ids), lambda: value
    ).reshape(-1)


def solution(mesh):
    in_specs = (P(("wide", "pair"), None), P(("wide", "pair")))
    out_specs = P(("wide", "pair"))
    return jax.shard_map(
        per_device, mesh=mesh, in_specs=in_specs, out_specs=out_specs, check_vma=False
    )
```

```python
import functools

import jax
import jax.numpy as jnp
from jax import lax
from jax.experimental import pallas as pl
from jax.experimental.pallas import tpu as pltpu
from jax.sharding import PartitionSpec as P

EPSILON = 1e-06
OWNERS = 16
CAP = 64
HALF = CAP // 2
CHUNK = OWNERS * HALF
SHORT = 208
LOW = -1e30
MARK = 2.0
F32 = jnp.float32
BF16 = jnp.bfloat16


def params():
    return pltpu.CompilerParams(vmem_limit_bytes=24 * 1024 * 1024)


def cost(flops, bytes_accessed):
    return pl.CostEstimate(flops=flops, bytes_accessed=bytes_accessed, transcendentals=0)


def iota(shape, dim):
    return lax.broadcasted_iota(jnp.int32, shape, dim)


def marked(head):
    return head.astype(F32)[:, 0:1] > 1.5


def place(half, unit, ids, rank, out_ref):
    rows = unit.shape[0]
    inside = (rank >= half * HALF) & (rank < (half + 1) * HALF)
    slot = jnp.where(inside, ids * HALF + rank - half * HALF, -1)
    onehot = (iota((CHUNK, rows), 0) == slot).astype(BF16)
    moved = jnp.dot(onehot, unit, preferred_element_type=F32)
    taken = jnp.dot(onehot, jnp.ones((rows, 128), BF16), preferred_element_type=F32)
    out_ref[...] = moved.astype(BF16)
    mark = jnp.where(iota((CHUNK, 128), 1) == 0, MARK * (1.0 - taken), 0.0)
    out_ref[:, 0:128] = (moved[:, 0:128] + mark).astype(BF16)


def prep_kernel(x_hbm, ids_hbm, first_ref, unit_ref, meta_ref, x_ref, ids_ref, sems):
    rows = x_ref.shape[0]
    parts = 4
    step = rows // parts
    copies = [pltpu.make_async_copy(ids_hbm, ids_ref, sems.at[parts])]
    for i in range(parts):
        at = pl.ds(i * step, step)
        copies.append(pltpu.make_async_copy(x_hbm.at[at], x_ref.at[at], sems.at[i]))
    for copy in copies:
        copy.start()
    copies[0].wait()
    ids = ids_ref[...]
    onehot = iota((OWNERS, rows), 0) == ids
    upto = (iota((rows, rows), 0) <= iota((rows, rows), 1)).astype(BF16)
    counts = jnp.dot(onehot.astype(BF16), upto, preferred_element_type=F32)
    rank = jnp.sum(jnp.where(onehot, counts, 0.0), axis=0, keepdims=True).astype(jnp.int32) - 1
    meta_ref[...] = jnp.where(iota((8, rows), 0) == 0, ids, rank)
    for i in range(parts):
        copies[i + 1].wait()
        at = pl.ds(i * step, step)
        x = x_ref[at, :]
        scale = lax.rsqrt(jnp.sum(x * x, axis=1, keepdims=True) + EPSILON)
        unit_ref[at, :] = (x * scale).astype(BF16)
    place(0, unit_ref[...], ids, rank, first_ref)


def prep(embeddings, ids):
    rows, width = embeddings.shape
    return pl.pallas_call(
        prep_kernel,
        in_specs=[pl.BlockSpec(memory_space=pltpu.HBM)] * 2,
        out_shape=(
            jax.ShapeDtypeStruct((CHUNK, width), BF16),
            jax.ShapeDtypeStruct((rows, width), BF16),
            jax.ShapeDtypeStruct((8, rows), jnp.int32),
        ),
        scratch_shapes=[
            pltpu.VMEM((rows, width), F32),
            pltpu.VMEM((1, rows), jnp.int32),
            pltpu.SemaphoreType.DMA((5,)),
        ],
        compiler_params=params(),
        cost_estimate=cost(2 * CHUNK * rows * width, 8 * rows * width),
        name="prep",
    )(embeddings, ids)


def rest_kernel(unit_ref, meta_ref, second_ref):
    place(1, unit_ref[...], meta_ref[0:1, :], meta_ref[1:2, :], second_ref)


def rest(unit, meta):
    rows, width = unit.shape
    return pl.pallas_call(
        rest_kernel,
        out_shape=jax.ShapeDtypeStruct((CHUNK, width), BF16),
        compiler_params=params(),
        cost_estimate=cost(2 * CHUNK * rows * width, 4 * rows * width),
        name="rest",
    )(unit, meta)


def pack_kernel(block_ref, packed_ref, onehot_ref):
    rows = block_ref.shape[0]
    full = jnp.where(marked(block_ref[:, 0:128]), 0.0, 1.0)
    full = jnp.transpose(jnp.broadcast_to(full, (rows, 128)))[0:8, :]
    upto = (iota((rows, rows), 0) <= iota((rows, rows), 1)).astype(BF16)
    count = jnp.dot(full.astype(BF16), upto, preferred_element_type=F32)
    spot = jnp.where(full > 0.5, count - 1.0, -1.0).astype(jnp.int32)
    onehot = (iota((SHORT, rows), 0) == spot[0:1, :]).astype(BF16)
    onehot_ref[...] = onehot
    moved = jnp.dot(onehot, block_ref[...], preferred_element_type=F32)
    taken = jnp.dot(onehot, jnp.ones((rows, 128), BF16), preferred_element_type=F32)
    packed_ref[...] = moved.astype(BF16)
    mark = jnp.where(iota((SHORT, 128), 1) == 0, MARK * (1.0 - taken), 0.0)
    packed_ref[:, 0:128] = (moved[:, 0:128] + mark).astype(BF16)


def pack(block):
    rows, width = block.shape
    return pl.pallas_call(
        pack_kernel,
        out_shape=(
            jax.ShapeDtypeStruct((SHORT, width), BF16),
            jax.ShapeDtypeStruct((SHORT, rows), BF16),
        ),
        compiler_params=params(),
        cost_estimate=cost(2 * SHORT * rows * width, 4 * rows * width),
        name="pack",
    )(block)


def lanes(rows):
    return -(-rows // 128) * 128


def pair_kernel(units, n_blocks, n_before, wanted, tails, *refs):
    blocks = refs[:n_blocks]
    before = refs[n_blocks : n_blocks + n_before]
    outs = refs[n_blocks + n_before : n_blocks + n_before + len(wanted)]
    lane_bias, row_bias, over_lanes, over_rows = refs[n_blocks + n_before + len(wanted) :]
    lefts = sorted({left for left, _, _ in units})
    rights = sorted({right for _, right, mode in units if mode == "both"})
    for b in sorted({b for unit in units for b in unit[0:2]}):
        rows = blocks[b].shape[0]
        bias = jnp.where(marked(blocks[b][:, 0:128]), LOW, 0.0)
        lane_bias[b, 0:rows] = jnp.broadcast_to(bias, (rows, 128))
        if any(b == right for _, right, _ in units):
            turned = jnp.transpose(lane_bias[b, 0 : lanes(rows)])
            row_bias[b, :, 0 : lanes(rows)] = turned[0:8, :]
        if b in lefts:
            over_lanes[b, 0 : lanes(rows)] = jnp.full((lanes(rows), 128), LOW, F32)
        if b in rights:
            over_rows[b, :, 0 : lanes(rows)] = jnp.full((8, lanes(rows)), LOW, F32)
    for left, right, mode in units:
        n_left, n_right = blocks[left].shape[0], blocks[right].shape[0]
        scores = lax.dot_general(
            blocks[left][...], blocks[right][...], (((1,), (1,)), ((), ())), preferred_element_type=F32
        )
        valid = scores + row_bias[right, 0:1, 0:n_right]
        if mode == "self":
            valid = jnp.where(iota(scores.shape, 0) == iota(scores.shape, 1), LOW, valid)
        best = over_lanes[left, 0:n_left]
        whole_groups = n_right // 128 * 128
        for g in range(0, whole_groups, 128):
            best = jnp.maximum(best, valid[:, g : g + 128])
        over_lanes[left, 0:n_left] = best
        if whole_groups < n_right:
            some = n_right - whole_groups
            best = jnp.maximum(over_lanes[left, 0:n_left, 0:some], valid[:, whole_groups:])
            over_lanes[left, 0:n_left, 0:some] = best
        if mode == "both":
            bias = lane_bias[left, 0:n_left]
            for g in range(0, n_right, 128):
                end = min(g + 128, n_right)
                part = scores[:, g:end] + bias[:, 0 : end - g]
                part = jnp.max(part.reshape(n_left // 8, 8, end - g), axis=0)
                over_rows[right, :, g:end] = jnp.maximum(over_rows[right, :, g:end], part)
    flag = jnp.zeros((1, 128), F32)
    for b in tails:
        end = blocks[b].shape[0]
        last = blocks[b][end - 16 : end, 0:128].astype(F32)[15:16, 0:1]
        flag = jnp.maximum(flag, jnp.where(last > 1.5, 0.0, 1.0))
    for (first, second, earlier), out in zip(wanted, outs):
        for b, at, n in ((first, 0, CHUNK), (second, CHUNK, out.shape[1] - CHUNK - 128)):
            part = jnp.full((1, n), LOW, F32)
            if b in lefts:
                part = jnp.max(jnp.transpose(over_lanes[b, 0:n]), axis=0, keepdims=True)
            if b in rights:
                part = jnp.maximum(part, jnp.max(over_rows[b, :, 0:n], axis=0, keepdims=True))
            for e in earlier:
                part = jnp.maximum(part, before[e][:, at : at + n])
            out[:, at : at + n] = part
        out[:, out.shape[1] - 128 :] = flag


def pairs(units, blocks, before, wanted, tails, width, name):
    n = len(blocks)
    rows, depth = blocks[0].shape
    work = sum(blocks[a].shape[0] * blocks[b].shape[0] for a, b, _ in units)
    return pl.pallas_call(
        functools.partial(pair_kernel, units, n, len(before), wanted, tails),
        out_shape=tuple(jax.ShapeDtypeStruct((1, width + 128), F32) for _ in wanted),
        scratch_shapes=[
            pltpu.VMEM((n, rows, 128), F32),
            pltpu.VMEM((n, 8, rows), F32),
            pltpu.VMEM((n, rows, 128), F32),
            pltpu.VMEM((n, 8, rows), F32),
        ],
        compiler_params=params(),
        cost_estimate=cost(2 * work * depth, 2 * n * rows * depth),
        name=name,
    )(*blocks, *before)


def three_parts(value):
    parts = []
    for _ in range(3):
        part = value.astype(BF16).astype(F32)
        value = value - part
        parts.append(part)
    return jnp.concatenate(parts, axis=0).astype(BF16)


def join_kernel(packed, own_ref, a_ref, b_ref, *rest):
    best = jnp.maximum(jnp.maximum(own_ref[...], a_ref[...]), jnp.maximum(b_ref[...], -1.0))
    out_ref = rest[-1]
    second = best[:, CHUNK:-128]
    if packed:
        parts = three_parts(jnp.broadcast_to(second[:, 0:SHORT], (8, SHORT)))
        moved = jnp.dot(parts, rest[0][...], preferred_element_type=F32)
        second = moved[0:1, :] + moved[8:9, :] + moved[16:17, :]
    for source in range(OWNERS):
        at = source * HALF
        row = slice(source, source + 1)
        out_ref[row, 0:HALF] = best[:, at : at + HALF]
        out_ref[row, HALF:CAP] = second[:, at : at + HALF]
        out_ref[row, CAP:128] = best[:, -CAP:]


def join(own, a, b, *onehot):
    return pl.pallas_call(
        functools.partial(join_kernel, bool(onehot)),
        out_shape=jax.ShapeDtypeStruct((OWNERS, 128), F32),
        compiler_params=params(),
        name="join",
    )(own, a, b, *onehot)


def pick_kernel(back_ref, meta_ref, out_ref, flag_ref):
    rows = meta_ref.shape[1]
    ids = meta_ref[0:1, :]
    rank = meta_ref[1:2, :]
    flag_ref[...] = jnp.max(jnp.max(back_ref[:, CAP:], axis=0, keepdims=True), axis=1, keepdims=True)
    onehot = ((iota((3 * OWNERS, rows), 0) & (OWNERS - 1)) == ids).astype(BF16)
    tiles = back_ref[...]
    moved = lax.dot_general(
        three_parts(tiles), onehot, (((0,), (0,)), ((), ())), preferred_element_type=F32
    )[0:CAP, :]
    out_ref[...] = jnp.sum(jnp.where(iota((CAP, rows), 0) == rank, moved, 0.0), axis=0, keepdims=True)


def pick(back, meta):
    return pl.pallas_call(
        pick_kernel,
        out_shape=(
            jax.ShapeDtypeStruct((1, meta.shape[1]), F32),
            jax.ShapeDtypeStruct((1, 1), F32),
        ),
        compiler_params=params(),
        name="pick",
    )(back, meta)


def swap_cores():
    return [(2 * z + k, 2 * z + 1 - k) for z in range(4) for k in range(2)]


LAST_CROSS = (0, 1, 1, 1)


def from_next():
    return [
        (2 * ((z + 1) % 4) + (k ^ 1 ^ LAST_CROSS[(z + 1) % 4]), 2 * z + k)
        for z in range(4)
        for k in range(2)
    ]


def from_last():
    return [(2 * ((z + 3) % 4) + (k ^ LAST_CROSS[z]), 2 * z + k) for z in range(4) for k in range(2)]


def inverse(perm):
    return [(b, a) for a, b in perm]


def to_owners(block):
    shape = block.shape
    block = block.reshape(OWNERS, HALF, shape[1])
    return lax.all_to_all(block, "wide", split_axis=0, concat_axis=0, tiled=True).reshape(shape)


def along_pair(block, perm):
    return lax.ppermute(block, "pair", perm)


def give_back(own, nxt, last, meta, *onehot):
    tiles = join(
        own,
        along_pair(nxt, inverse(from_next())),
        along_pair(last, inverse(from_last())),
        *onehot,
    )
    back = lax.all_to_all(tiles.reshape(OWNERS, 1, 128), "wide", split_axis=0, concat_axis=0, tiled=True)
    return pick(back.reshape(OWNERS, 128), meta)


EARLY = (
    (0, 0, "self"), (0, 2, "left"), (0, 4, "both"), (0, 5, "both"), (5, 4, "both"),
    (0, 1, "both"), (1, 1, "self"), (0, 3, "left"), (1, 2, "left"), (1, 3, "left"),
    (1, 4, "both"), (1, 5, "both"), (3, 4, "both"), (3, 5, "both"),
)
LATE = ((5, 6, "both"), (7, 4, "both"), (1, 6, "both"), (1, 7, "both"), (7, 6, "both"))


def match(a, second, tails):
    own_a, sib_a, next_a, last_a = a
    own_b, sib_b, next_b, last_b = second
    width = CHUNK + lanes(own_b.shape[0])
    own, sib, nxt, last = pairs(
        EARLY,
        (own_a, own_b, sib_a, sib_b, next_a, last_a),
        (),
        ((0, 1, ()), (2, 3, ()), (4, None, ()), (5, None, ())),
        (),
        width,
        "early",
    )
    sib = along_pair(sib, swap_cores())
    return pairs(
        LATE,
        (own_a, own_b, sib_a, sib_b, next_a, last_a, next_b, last_b),
        (own, sib, nxt, last),
        ((0, 1, (0, 1)), (4, 6, (2,)), (5, 7, (3,))),
        tails,
        width,
        "late",
    )


def neighbours(block):
    return (
        block,
        along_pair(block, swap_cores()),
        along_pair(block, from_next()),
        along_pair(block, from_last()),
    )


def exchange(embeddings, ids):
    first, unit, meta = prep(embeddings, ids)
    own_a = to_owners(first)
    own_a, unit = lax.optimization_barrier((own_a, unit))
    a = neighbours(own_a)
    return a, to_owners(rest(unit, meta)), meta


def whole(embeddings, ids):
    a, own_b, meta = exchange(embeddings, ids)
    own_b, *a = lax.optimization_barrier((own_b, *a))
    best = match(a, neighbours(own_b), ())
    return give_back(*best, meta)[0]


def per_device(embeddings, cluster_ids):
    ids = cluster_ids.reshape(1, -1)
    a, own_b, meta = exchange(embeddings, ids)
    packed, onehot = pack(own_b)
    packed, *a = lax.optimization_barrier((packed, *a))
    best = match(a, neighbours(packed), (1, 3, 6, 7))
    value, flag = give_back(*best, meta, onehot)
    return lax.cond(
        flag.reshape(()) > 0.5, lambda: whole(embeddings, ids), lambda: value
    ).reshape(-1)


def solution(mesh):
    in_specs = (P(("wide", "pair"), None), P(("wide", "pair")))
    out_specs = P(("wide", "pair"))
    return jax.shard_map(
        per_device, mesh=mesh, in_specs=in_specs, out_specs=out_specs, check_vma=False
    )
```

```python
import functools

import jax
import jax.numpy as jnp
from jax import lax
from jax.experimental import pallas as pl
from jax.experimental.pallas import tpu as pltpu
from jax.sharding import PartitionSpec as P

EPSILON = 1e-06
OWNERS = 16
CAP = 64
HALF = CAP // 2
CHUNK = OWNERS * HALF
SHORT = 208
LOW = -1e30
MARK = 2.0
F32 = jnp.float32
BF16 = jnp.bfloat16


def params():
    return pltpu.CompilerParams(vmem_limit_bytes=24 * 1024 * 1024)


def cost(flops, bytes_accessed):
    return pl.CostEstimate(flops=flops, bytes_accessed=bytes_accessed, transcendentals=0)


def iota(shape, dim):
    return lax.broadcasted_iota(jnp.int32, shape, dim)


def marked(head):
    return head.astype(F32)[:, 0:1] > 1.5


def place(half, unit, ids, rank, out_ref):
    rows = unit.shape[0]
    inside = (rank >= half * HALF) & (rank < (half + 1) * HALF)
    slot = jnp.where(inside, ids * HALF + rank - half * HALF, -1)
    onehot = (iota((CHUNK, rows), 0) == slot).astype(BF16)
    moved = jnp.dot(onehot, unit, preferred_element_type=F32)
    taken = jnp.dot(onehot, jnp.ones((rows, 128), BF16), preferred_element_type=F32)
    out_ref[...] = moved.astype(BF16)
    mark = jnp.where(iota((CHUNK, 128), 1) == 0, MARK * (1.0 - taken), 0.0)
    out_ref[:, 0:128] = (moved[:, 0:128] + mark).astype(BF16)


def prep_kernel(x_hbm, ids_hbm, first_ref, unit_ref, meta_ref, x_ref, ids_ref, sems):
    rows = x_ref.shape[0]
    parts = 4
    step = rows // parts
    copies = [pltpu.make_async_copy(ids_hbm, ids_ref, sems.at[parts])]
    for i in range(parts):
        at = pl.ds(i * step, step)
        copies.append(pltpu.make_async_copy(x_hbm.at[at], x_ref.at[at], sems.at[i]))
    for copy in copies:
        copy.start()
    copies[0].wait()
    ids = ids_ref[...]
    onehot = iota((OWNERS, rows), 0) == ids
    upto = (iota((rows, rows), 0) <= iota((rows, rows), 1)).astype(BF16)
    counts = jnp.dot(onehot.astype(BF16), upto, preferred_element_type=F32)
    rank = jnp.sum(jnp.where(onehot, counts, 0.0), axis=0, keepdims=True).astype(jnp.int32) - 1
    meta_ref[...] = jnp.where(iota((8, rows), 0) == 0, ids, rank)
    for i in range(parts):
        copies[i + 1].wait()
        at = pl.ds(i * step, step)
        x = x_ref[at, :]
        scale = lax.rsqrt(jnp.sum(x * x, axis=1, keepdims=True) + EPSILON)
        unit_ref[at, :] = (x * scale).astype(BF16)
    place(0, unit_ref[...], ids, rank, first_ref)


def prep(embeddings, ids):
    rows, width = embeddings.shape
    return pl.pallas_call(
        prep_kernel,
        in_specs=[pl.BlockSpec(memory_space=pltpu.HBM)] * 2,
        out_shape=(
            jax.ShapeDtypeStruct((CHUNK, width), BF16),
            jax.ShapeDtypeStruct((rows, width), BF16),
            jax.ShapeDtypeStruct((8, rows), jnp.int32),
        ),
        scratch_shapes=[
            pltpu.VMEM((rows, width), F32),
            pltpu.VMEM((1, rows), jnp.int32),
            pltpu.SemaphoreType.DMA((5,)),
        ],
        compiler_params=params(),
        cost_estimate=cost(2 * CHUNK * rows * width, 8 * rows * width),
        name="prep",
    )(embeddings, ids)


def rest_kernel(unit_ref, meta_ref, second_ref, ranks_ref):
    ranks_ref[...] = (iota(ranks_ref.shape, 0) == meta_ref[1:2, :]).astype(BF16)
    place(1, unit_ref[...], meta_ref[0:1, :], meta_ref[1:2, :], second_ref)


def rest(unit, meta):
    rows, width = unit.shape
    return pl.pallas_call(
        rest_kernel,
        out_shape=(
            jax.ShapeDtypeStruct((CHUNK, width), BF16),
            jax.ShapeDtypeStruct((128, rows), BF16),
        ),
        compiler_params=params(),
        cost_estimate=cost(2 * CHUNK * rows * width, 4 * rows * width),
        name="rest",
    )(unit, meta)


def pack_kernel(block_ref, packed_ref, source_ref, spread_ref):
    rows = block_ref.shape[0]
    full = jnp.where(marked(block_ref[:, 0:128]), 0.0, 1.0)
    full = jnp.transpose(jnp.broadcast_to(full, (rows, 128)))[0:8, :]
    upto = (iota((rows, rows), 0) <= iota((rows, rows), 1)).astype(BF16)
    count = jnp.dot(full.astype(BF16), upto, preferred_element_type=F32)
    spot = jnp.where(full > 0.5, count - 1.0, -1.0).astype(jnp.int32)
    wide = (iota((lanes(SHORT), rows), 0) == spot[0:1, :]).astype(BF16)
    source = (iota((OWNERS, rows), 1) // HALF == iota((OWNERS, rows), 0)).astype(BF16)
    source_ref[...] = lax.dot_general(
        source, wide, (((1,), (1,)), ((), ())), preferred_element_type=F32
    )
    lane = (iota((rows, 128), 0) % HALF + HALF == iota((rows, 128), 1)).astype(BF16)
    spread_ref[...] = jnp.dot(wide, lane, preferred_element_type=F32).astype(BF16)
    onehot = wide[0:SHORT, :]
    moved = jnp.dot(onehot, block_ref[...], preferred_element_type=F32)
    taken = jnp.dot(onehot, jnp.ones((rows, 128), BF16), preferred_element_type=F32)
    packed_ref[...] = moved.astype(BF16)
    mark = jnp.where(iota((SHORT, 128), 1) == 0, MARK * (1.0 - taken), 0.0)
    packed_ref[:, 0:128] = (moved[:, 0:128] + mark).astype(BF16)


def pack(block):
    rows, width = block.shape
    return pl.pallas_call(
        pack_kernel,
        out_shape=(
            jax.ShapeDtypeStruct((SHORT, width), BF16),
            jax.ShapeDtypeStruct((OWNERS, lanes(SHORT)), F32),
            jax.ShapeDtypeStruct((lanes(SHORT), 128), BF16),
        ),
        compiler_params=params(),
        cost_estimate=cost(2 * SHORT * rows * width, 4 * rows * width),
        name="pack",
    )(block)


def lanes(rows):
    return -(-rows // 128) * 128


def pair_kernel(units, n_blocks, n_before, wanted, tails, *refs):
    blocks = refs[:n_blocks]
    before = refs[n_blocks : n_blocks + n_before]
    outs = refs[n_blocks + n_before : n_blocks + n_before + len(wanted)]
    lane_bias, row_bias, over_lanes, over_rows = refs[n_blocks + n_before + len(wanted) :]
    lefts = sorted({left for left, _, _ in units})
    rights = sorted({right for _, right, mode in units if mode == "both"})
    for b in sorted({b for unit in units for b in unit[0:2]}):
        rows = blocks[b].shape[0]
        bias = jnp.where(marked(blocks[b][:, 0:128]), LOW, 0.0)
        lane_bias[b, 0:rows] = jnp.broadcast_to(bias, (rows, 128))
        if any(b == right for _, right, _ in units):
            turned = jnp.transpose(lane_bias[b, 0 : lanes(rows)])
            row_bias[b, :, 0 : lanes(rows)] = turned[0:8, :]
        if b in lefts:
            over_lanes[b, 0 : lanes(rows)] = jnp.full((lanes(rows), 128), LOW, F32)
        if b in rights:
            over_rows[b, :, 0 : lanes(rows)] = jnp.full((8, lanes(rows)), LOW, F32)
    for left, right, mode in units:
        n_left, n_right = blocks[left].shape[0], blocks[right].shape[0]
        scores = lax.dot_general(
            blocks[left][...], blocks[right][...], (((1,), (1,)), ((), ())), preferred_element_type=F32
        )
        valid = scores + row_bias[right, 0:1, 0:n_right]
        if mode == "self":
            valid = jnp.where(iota(scores.shape, 0) == iota(scores.shape, 1), LOW, valid)
        best = over_lanes[left, 0:n_left]
        whole_groups = n_right // 128 * 128
        for g in range(0, whole_groups, 128):
            best = jnp.maximum(best, valid[:, g : g + 128])
        over_lanes[left, 0:n_left] = best
        if whole_groups < n_right:
            some = n_right - whole_groups
            best = jnp.maximum(over_lanes[left, 0:n_left, 0:some], valid[:, whole_groups:])
            over_lanes[left, 0:n_left, 0:some] = best
        if mode == "both":
            bias = lane_bias[left, 0:n_left]
            for g in range(0, n_right, 128):
                end = min(g + 128, n_right)
                part = scores[:, g:end] + bias[:, 0 : end - g]
                part = jnp.max(part.reshape(n_left // 8, 8, end - g), axis=0)
                over_rows[right, :, g:end] = jnp.maximum(over_rows[right, :, g:end], part)
    flag = jnp.zeros((1, 128), F32)
    for b in tails:
        end = blocks[b].shape[0]
        last = blocks[b][end - 16 : end, 0:128].astype(F32)[15:16, 0:1]
        flag = jnp.maximum(flag, jnp.where(last > 1.5, 0.0, 1.0))
    for (first, second, earlier), out in zip(wanted, outs):
        for b, at, n in ((first, 0, CHUNK), (second, CHUNK, out.shape[1] - CHUNK - 128)):
            part = jnp.full((1, n), LOW, F32)
            if b in lefts:
                part = jnp.max(jnp.transpose(over_lanes[b, 0:n]), axis=0, keepdims=True)
            if b in rights:
                part = jnp.maximum(part, jnp.max(over_rows[b, :, 0:n], axis=0, keepdims=True))
            for e in earlier:
                part = jnp.maximum(part, before[e][:, at : at + n])
            out[:, at : at + n] = part
        out[:, out.shape[1] - 128 :] = flag


def pairs(units, blocks, before, wanted, tails, width, name):
    n = len(blocks)
    rows, depth = blocks[0].shape
    work = sum(blocks[a].shape[0] * blocks[b].shape[0] for a, b, _ in units)
    return pl.pallas_call(
        functools.partial(pair_kernel, units, n, len(before), wanted, tails),
        out_shape=tuple(jax.ShapeDtypeStruct((1, width + 128), F32) for _ in wanted),
        scratch_shapes=[
            pltpu.VMEM((n, rows, 128), F32),
            pltpu.VMEM((n, 8, rows), F32),
            pltpu.VMEM((n, rows, 128), F32),
            pltpu.VMEM((n, 8, rows), F32),
        ],
        compiler_params=params(),
        cost_estimate=cost(2 * work * depth, 2 * n * rows * depth),
        name=name,
    )(*blocks, *before)


def three_parts(value):
    parts = []
    for _ in range(3):
        part = value.astype(BF16).astype(F32)
        value = value - part
        parts.append(part)
    return jnp.concatenate(parts, axis=0).astype(BF16)


def join_kernel(packed, own_ref, a_ref, b_ref, *rest):
    best = jnp.maximum(jnp.maximum(own_ref[...], a_ref[...]), jnp.maximum(b_ref[...], -1.0))
    out_ref = rest[-1]
    second = best[:, CHUNK:-128]
    if packed:
        source_ref, spread_ref = rest[:2]
        value = jnp.where(source_ref[...] > 0.5, second, 0.0)
        moved = jnp.dot(three_parts(value), spread_ref[...], preferred_element_type=F32)
        out_ref[...] = moved[0:OWNERS] + moved[OWNERS : 2 * OWNERS] + moved[2 * OWNERS :]
    for source in range(OWNERS):
        at = source * HALF
        row = slice(source, source + 1)
        out_ref[row, 0:HALF] = best[:, at : at + HALF]
        if not packed:
            out_ref[row, HALF:CAP] = second[:, at : at + HALF]
        out_ref[row, CAP:128] = best[:, -CAP:]


def join(own, a, b, *moves):
    return pl.pallas_call(
        functools.partial(join_kernel, bool(moves)),
        out_shape=pltpu.VMEM((OWNERS, 128), F32),
        compiler_params=params(),
        name="join",
    )(own, a, b, *moves)


def pick_kernel(back_ref, meta_ref, ranks_ref, out_ref, flag_ref):
    rows = meta_ref.shape[1]
    tiles = back_ref[...]
    moved = jnp.dot(three_parts(tiles), ranks_ref[...], preferred_element_type=F32)
    moved = moved[0:OWNERS] + moved[OWNERS : 2 * OWNERS] + moved[2 * OWNERS :]
    mine = iota((OWNERS, rows), 0) == meta_ref[0:1, :]
    out_ref[...] = jnp.sum(jnp.where(mine, moved, 0.0), axis=0, keepdims=True)
    flag_ref[0, 0] = (jnp.max(tiles[:, CAP:]) > 0.5).astype(jnp.int32)


def pick(back, meta, ranks):
    return pl.pallas_call(
        pick_kernel,
        out_shape=(
            jax.ShapeDtypeStruct((1, meta.shape[1]), F32),
            pltpu.SMEM((1, 1), jnp.int32),
        ),
        out_specs=(
            pl.BlockSpec(memory_space=pltpu.VMEM),
            pl.BlockSpec(memory_space=pltpu.SMEM),
        ),
        compiler_params=params(),
        name="pick",
    )(back, meta, ranks)


def swap_cores():
    return [(2 * z + k, 2 * z + 1 - k) for z in range(4) for k in range(2)]


LAST_CROSS = (0, 1, 1, 1)


def from_next():
    return [
        (2 * ((z + 1) % 4) + (k ^ 1 ^ LAST_CROSS[(z + 1) % 4]), 2 * z + k)
        for z in range(4)
        for k in range(2)
    ]


def from_last():
    return [(2 * ((z + 3) % 4) + (k ^ LAST_CROSS[z]), 2 * z + k) for z in range(4) for k in range(2)]


def inverse(perm):
    return [(b, a) for a, b in perm]


def to_owners(block):
    shape = block.shape
    block = block.reshape(OWNERS, HALF, shape[1])
    return lax.all_to_all(block, "wide", split_axis=0, concat_axis=0, tiled=True).reshape(shape)


def along_pair(block, perm):
    return lax.ppermute(block, "pair", perm)


def give_back(own, nxt, last, own_rows, *moves):
    tiles = join(
        own,
        along_pair(nxt, inverse(from_next())),
        along_pair(last, inverse(from_last())),
        *moves,
    )
    back = lax.all_to_all(tiles.reshape(OWNERS, 1, 128), "wide", split_axis=0, concat_axis=0, tiled=True)
    return pick(back.reshape(OWNERS, 128), *own_rows)


EARLY = (
    (0, 0, "self"), (0, 2, "left"), (0, 4, "both"), (0, 5, "both"), (5, 4, "both"),
    (0, 1, "both"), (1, 1, "self"), (0, 3, "left"), (1, 2, "left"), (1, 3, "left"),
    (1, 4, "both"), (1, 5, "both"), (3, 4, "both"), (3, 5, "both"),
)
LATE = ((5, 6, "both"), (7, 4, "both"), (1, 6, "both"), (1, 7, "both"), (7, 6, "both"))


def match(a, second, tails):
    own_a, sib_a, next_a, last_a = a
    own_b, sib_b, next_b, last_b = second
    width = CHUNK + lanes(own_b.shape[0])
    own, sib, nxt, last = pairs(
        EARLY,
        (own_a, own_b, sib_a, sib_b, next_a, last_a),
        (),
        ((0, 1, ()), (2, 3, ()), (4, None, ()), (5, None, ())),
        (),
        width,
        "early",
    )
    sib = along_pair(sib, swap_cores())
    return pairs(
        LATE,
        (own_a, own_b, sib_a, sib_b, next_a, last_a, next_b, last_b),
        (own, sib, nxt, last),
        ((0, 1, (0, 1)), (4, 6, (2,)), (5, 7, (3,))),
        tails,
        width,
        "late",
    )


def neighbours(block):
    return (
        block,
        along_pair(block, swap_cores()),
        along_pair(block, from_next()),
        along_pair(block, from_last()),
    )


def exchange(embeddings, ids):
    first, unit, meta = prep(embeddings, ids)
    own_a = to_owners(first)
    own_a, unit = lax.optimization_barrier((own_a, unit))
    a = neighbours(own_a)
    second, ranks = rest(unit, meta)
    return a, to_owners(second), (meta, ranks)


def whole(embeddings, ids, a, own_b):
    _, unit, meta = prep(embeddings, ids)
    _, ranks = rest(unit, meta)
    best = match(a, neighbours(own_b), ())
    return give_back(*best, (meta, ranks))[0]


def per_device(embeddings, cluster_ids):
    ids = cluster_ids.reshape(1, -1)
    a, own_b, own_rows = exchange(embeddings, ids)
    packed, *moves = pack(own_b)
    packed, *a = lax.optimization_barrier((packed, *a))
    best = match(a, neighbours(packed), (1, 3, 6, 7))
    value, flag = give_back(*best, own_rows, *moves)
    return lax.cond(
        flag.reshape(()) != 0, lambda: whole(embeddings, ids, a, own_b), lambda: value
    ).reshape(-1)


def solution(mesh):
    in_specs = (P(("wide", "pair"), None), P(("wide", "pair")))
    out_specs = P(("wide", "pair"))
    return jax.shard_map(
        per_device, mesh=mesh, in_specs=in_specs, out_specs=out_specs, check_vma=False
    )
```

```python
import functools

import jax
import jax.numpy as jnp
from jax import lax
from jax.experimental import pallas as pl
from jax.experimental.pallas import tpu as pltpu
from jax.sharding import PartitionSpec as P

EPSILON = 1e-06
OWNERS = 16
CAP = 64
HALF = CAP // 2
CHUNK = OWNERS * HALF
SHORT = 208
LOW = -1e30
MARK = 2.0
F32 = jnp.float32
BF16 = jnp.bfloat16


def params():
    return pltpu.CompilerParams(vmem_limit_bytes=24 * 1024 * 1024)


def cost(flops, bytes_accessed):
    return pl.CostEstimate(flops=flops, bytes_accessed=bytes_accessed, transcendentals=0)


def iota(shape, dim):
    return lax.broadcasted_iota(jnp.int32, shape, dim)


def marked(head):
    return head.astype(F32)[:, 0:1] > 1.5


def place(half, unit, ids, rank, out_ref):
    rows = unit.shape[0]
    inside = (rank >= half * HALF) & (rank < (half + 1) * HALF)
    slot = jnp.where(inside, ids * HALF + rank - half * HALF, -1)
    onehot = (iota((CHUNK, rows), 0) == slot).astype(BF16)
    moved = jnp.dot(onehot, unit, preferred_element_type=F32)
    taken = jnp.dot(onehot, jnp.ones((rows, 128), BF16), preferred_element_type=F32)
    out_ref[...] = moved.astype(BF16)
    mark = jnp.where(iota((CHUNK, 128), 1) == 0, MARK * (1.0 - taken), 0.0)
    out_ref[:, 0:128] = (moved[:, 0:128] + mark).astype(BF16)


def prep_kernel(x_hbm, ids_hbm, first_ref, unit_ref, meta_ref, x_ref, ids_ref, sems):
    rows = x_ref.shape[0]
    parts = 4
    step = rows // parts
    copies = [pltpu.make_async_copy(ids_hbm, ids_ref, sems.at[parts])]
    for i in range(parts):
        at = pl.ds(i * step, step)
        copies.append(pltpu.make_async_copy(x_hbm.at[at], x_ref.at[at], sems.at[i]))
    for copy in copies:
        copy.start()
    copies[0].wait()
    ids = ids_ref[...]
    onehot = iota((OWNERS, rows), 0) == ids
    upto = (iota((rows, rows), 0) <= iota((rows, rows), 1)).astype(BF16)
    counts = jnp.dot(onehot.astype(BF16), upto, preferred_element_type=F32)
    rank = jnp.sum(jnp.where(onehot, counts, 0.0), axis=0, keepdims=True).astype(jnp.int32) - 1
    meta_ref[...] = jnp.where(iota((8, rows), 0) == 0, ids, rank)
    for i in range(parts):
        copies[i + 1].wait()
        at = pl.ds(i * step, step)
        x = x_ref[at, :]
        scale = lax.rsqrt(jnp.sum(x * x, axis=1, keepdims=True) + EPSILON)
        unit_ref[at, :] = (x * scale).astype(BF16)
    place(0, unit_ref[...], ids, rank, first_ref)


def prep(embeddings, ids):
    rows, width = embeddings.shape
    return pl.pallas_call(
        prep_kernel,
        in_specs=[pl.BlockSpec(memory_space=pltpu.HBM)] * 2,
        out_shape=(
            jax.ShapeDtypeStruct((CHUNK, width), BF16),
            jax.ShapeDtypeStruct((rows, width), BF16),
            jax.ShapeDtypeStruct((8, rows), jnp.int32),
        ),
        scratch_shapes=[
            pltpu.VMEM((rows, width), F32),
            pltpu.VMEM((1, rows), jnp.int32),
            pltpu.SemaphoreType.DMA((5,)),
        ],
        compiler_params=params(),
        cost_estimate=cost(2 * CHUNK * rows * width, 8 * rows * width),
        name="prep",
    )(embeddings, ids)


def rest_kernel(unit_ref, meta_ref, second_ref):
    place(1, unit_ref[...], meta_ref[0:1, :], meta_ref[1:2, :], second_ref)


def rest(unit, meta):
    rows, width = unit.shape
    return pl.pallas_call(
        rest_kernel,
        out_shape=jax.ShapeDtypeStruct((CHUNK, width), BF16),
        compiler_params=params(),
        cost_estimate=cost(2 * CHUNK * rows * width, 4 * rows * width),
        name="rest",
    )(unit, meta)


def pack_kernel(block_ref, packed_ref, spot_ref):
    rows = block_ref.shape[0]
    full = jnp.where(marked(block_ref[:, 0:128]), 0.0, 1.0)
    full = jnp.transpose(jnp.broadcast_to(full, (rows, 128)))[0:8, :]
    upto = (iota((rows, rows), 0) <= iota((rows, rows), 1)).astype(BF16)
    count = jnp.dot(full.astype(BF16), upto, preferred_element_type=F32)
    spot = jnp.where(full > 0.5, count - 1.0, -1.0).astype(jnp.int32)
    spot_ref[...] = spot
    onehot = (iota((SHORT, rows), 0) == spot[0:1, :]).astype(BF16)
    moved = jnp.dot(onehot, block_ref[...], preferred_element_type=F32)
    taken = jnp.dot(onehot, jnp.ones((rows, 128), BF16), preferred_element_type=F32)
    packed_ref[...] = moved.astype(BF16)
    mark = jnp.where(iota((SHORT, 128), 1) == 0, MARK * (1.0 - taken), 0.0)
    packed_ref[:, 0:128] = (moved[:, 0:128] + mark).astype(BF16)


def pack(block):
    rows, width = block.shape
    return pl.pallas_call(
        pack_kernel,
        out_shape=(
            jax.ShapeDtypeStruct((SHORT, width), BF16),
            jax.ShapeDtypeStruct((8, rows), jnp.int32),
        ),
        compiler_params=params(),
        cost_estimate=cost(2 * SHORT * rows * width, 4 * rows * width),
        name="pack",
    )(block)


def lanes(rows):
    return -(-rows // 128) * 128


def moves_kernel(spot_ref, source_ref, spread_ref):
    rows = spot_ref.shape[1]
    onehot = (iota((lanes(SHORT), rows), 0) == spot_ref[0:1, :]).astype(BF16)
    source = (iota((OWNERS, rows), 1) // HALF == iota((OWNERS, rows), 0)).astype(BF16)
    source_ref[...] = lax.dot_general(
        source, onehot, (((1,), (1,)), ((), ())), preferred_element_type=F32
    )
    lane = (iota((rows, 128), 0) % HALF + HALF == iota((rows, 128), 1)).astype(BF16)
    spread_ref[...] = jnp.dot(onehot, lane, preferred_element_type=F32).astype(BF16)


def moves_of(spot):
    return pl.pallas_call(
        moves_kernel,
        out_shape=(
            jax.ShapeDtypeStruct((OWNERS, lanes(SHORT)), F32),
            jax.ShapeDtypeStruct((lanes(SHORT), 128), BF16),
        ),
        compiler_params=params(),
        cost_estimate=cost(2 * lanes(SHORT) * spot.shape[1] * 256, 1 << 20),
        name="moves",
    )(spot)


def ranks_kernel(meta_ref, ranks_ref):
    ranks_ref[...] = (iota(ranks_ref.shape, 0) == meta_ref[1:2, :]).astype(BF16)


def ranks_of(meta):
    return pl.pallas_call(
        ranks_kernel,
        out_shape=jax.ShapeDtypeStruct((128, meta.shape[1]), BF16),
        compiler_params=params(),
        cost_estimate=cost(1 << 16, 1 << 17),
        name="ranks",
    )(meta)


def pair_kernel(units, n_blocks, n_before, wanted, tails, *refs):
    blocks = refs[:n_blocks]
    before = refs[n_blocks : n_blocks + n_before]
    outs = refs[n_blocks + n_before : n_blocks + n_before + len(wanted)]
    lane_bias, row_bias, over_lanes, over_rows = refs[n_blocks + n_before + len(wanted) :]
    lefts = sorted({left for left, _, _ in units})
    rights = sorted({right for _, right, mode in units if mode == "both"})
    for b in sorted({b for unit in units for b in unit[0:2]}):
        rows = blocks[b].shape[0]
        bias = jnp.where(marked(blocks[b][:, 0:128]), LOW, 0.0)
        lane_bias[b, 0:rows] = jnp.broadcast_to(bias, (rows, 128))
        if any(b == right for _, right, _ in units):
            turned = jnp.transpose(lane_bias[b, 0 : lanes(rows)])
            row_bias[b, :, 0 : lanes(rows)] = turned[0:8, :]
        if b in lefts:
            over_lanes[b, 0 : lanes(rows)] = jnp.full((lanes(rows), 128), LOW, F32)
        if b in rights:
            over_rows[b, :, 0 : lanes(rows)] = jnp.full((8, lanes(rows)), LOW, F32)
    for left, right, mode in units:
        n_left, n_right = blocks[left].shape[0], blocks[right].shape[0]
        scores = lax.dot_general(
            blocks[left][...], blocks[right][...], (((1,), (1,)), ((), ())), preferred_element_type=F32
        )
        valid = scores + row_bias[right, 0:1, 0:n_right]
        if mode == "self":
            valid = jnp.where(iota(scores.shape, 0) == iota(scores.shape, 1), LOW, valid)
        best = over_lanes[left, 0:n_left]
        whole_groups = n_right // 128 * 128
        for g in range(0, whole_groups, 128):
            best = jnp.maximum(best, valid[:, g : g + 128])
        over_lanes[left, 0:n_left] = best
        if whole_groups < n_right:
            some = n_right - whole_groups
            best = jnp.maximum(over_lanes[left, 0:n_left, 0:some], valid[:, whole_groups:])
            over_lanes[left, 0:n_left, 0:some] = best
        if mode == "both":
            bias = lane_bias[left, 0:n_left]
            for g in range(0, n_right, 128):
                end = min(g + 128, n_right)
                part = scores[:, g:end] + bias[:, 0 : end - g]
                part = jnp.max(part.reshape(n_left // 8, 8, end - g), axis=0)
                over_rows[right, :, g:end] = jnp.maximum(over_rows[right, :, g:end], part)
    flag = jnp.zeros((1, 128), F32)
    for b in tails:
        end = blocks[b].shape[0]
        last = blocks[b][end - 16 : end, 0:128].astype(F32)[15:16, 0:1]
        flag = jnp.maximum(flag, jnp.where(last > 1.5, 0.0, 1.0))
    for (first, second, earlier), out in zip(wanted, outs):
        for b, at, n in ((first, 0, CHUNK), (second, CHUNK, out.shape[1] - CHUNK - 128)):
            part = jnp.full((1, n), LOW, F32)
            if b in lefts:
                part = jnp.max(jnp.transpose(over_lanes[b, 0:n]), axis=0, keepdims=True)
            if b in rights:
                part = jnp.maximum(part, jnp.max(over_rows[b, :, 0:n], axis=0, keepdims=True))
            for e in earlier:
                part = jnp.maximum(part, before[e][:, at : at + n])
            out[:, at : at + n] = part
        out[:, out.shape[1] - 128 :] = flag


def pairs(units, blocks, before, wanted, tails, width, name):
    n = len(blocks)
    rows, depth = blocks[0].shape
    work = sum(blocks[a].shape[0] * blocks[b].shape[0] for a, b, _ in units)
    return pl.pallas_call(
        functools.partial(pair_kernel, units, n, len(before), wanted, tails),
        out_shape=tuple(jax.ShapeDtypeStruct((1, width + 128), F32) for _ in wanted),
        scratch_shapes=[
            pltpu.VMEM((n, rows, 128), F32),
            pltpu.VMEM((n, 8, rows), F32),
            pltpu.VMEM((n, rows, 128), F32),
            pltpu.VMEM((n, 8, rows), F32),
        ],
        compiler_params=params(),
        cost_estimate=cost(2 * work * depth, 2 * n * rows * depth),
        name=name,
    )(*blocks, *before)


def three_parts(value):
    parts = []
    for _ in range(3):
        part = value.astype(BF16).astype(F32)
        value = value - part
        parts.append(part)
    return jnp.concatenate(parts, axis=0).astype(BF16)


def join_kernel(packed, own_ref, a_ref, b_ref, *rest):
    best = jnp.maximum(jnp.maximum(own_ref[...], a_ref[...]), jnp.maximum(b_ref[...], -1.0))
    out_ref = rest[-1]
    second = best[:, CHUNK:-128]
    if packed:
        source_ref, spread_ref = rest[:2]
        value = jnp.where(source_ref[...] > 0.5, second, 0.0)
        moved = jnp.dot(three_parts(value), spread_ref[...], preferred_element_type=F32)
        out_ref[...] = moved[0:OWNERS] + moved[OWNERS : 2 * OWNERS] + moved[2 * OWNERS :]
    for source in range(OWNERS):
        at = source * HALF
        row = slice(source, source + 1)
        out_ref[row, 0:HALF] = best[:, at : at + HALF]
        if not packed:
            out_ref[row, HALF:CAP] = second[:, at : at + HALF]
        out_ref[row, CAP:128] = best[:, -CAP:]


def join(own, a, b, *moves):
    return pl.pallas_call(
        functools.partial(join_kernel, bool(moves)),
        out_shape=pltpu.VMEM((OWNERS, 128), F32),
        compiler_params=params(),
        name="join",
    )(own, a, b, *moves)


def pick_kernel(back_ref, meta_ref, ranks_ref, out_ref, flag_ref):
    rows = meta_ref.shape[1]
    tiles = back_ref[...]
    moved = jnp.dot(three_parts(tiles), ranks_ref[...], preferred_element_type=F32)
    moved = moved[0:OWNERS] + moved[OWNERS : 2 * OWNERS] + moved[2 * OWNERS :]
    mine = iota((OWNERS, rows), 0) == meta_ref[0:1, :]
    out_ref[...] = jnp.sum(jnp.where(mine, moved, 0.0), axis=0, keepdims=True)
    flag_ref[0, 0] = (jnp.max(tiles[:, CAP:]) > 0.5).astype(jnp.int32)


def pick(back, meta, ranks):
    return pl.pallas_call(
        pick_kernel,
        out_shape=(
            jax.ShapeDtypeStruct((1, meta.shape[1]), F32),
            pltpu.SMEM((1, 1), jnp.int32),
        ),
        out_specs=(
            pl.BlockSpec(memory_space=pltpu.VMEM),
            pl.BlockSpec(memory_space=pltpu.SMEM),
        ),
        compiler_params=params(),
        name="pick",
    )(back, meta, ranks)


def swap_cores():
    return [(2 * z + k, 2 * z + 1 - k) for z in range(4) for k in range(2)]


LAST_CROSS = (0, 1, 1, 1)


def from_next():
    return [
        (2 * ((z + 1) % 4) + (k ^ 1 ^ LAST_CROSS[(z + 1) % 4]), 2 * z + k)
        for z in range(4)
        for k in range(2)
    ]


def from_last():
    return [(2 * ((z + 3) % 4) + (k ^ LAST_CROSS[z]), 2 * z + k) for z in range(4) for k in range(2)]


def inverse(perm):
    return [(b, a) for a, b in perm]


def to_owners(block):
    shape = block.shape
    block = block.reshape(OWNERS, HALF, shape[1])
    return lax.all_to_all(block, "wide", split_axis=0, concat_axis=0, tiled=True).reshape(shape)


def along_pair(block, perm):
    return lax.ppermute(block, "pair", perm)


def give_back(own, nxt, last, own_rows, *moves):
    tiles = join(
        own,
        along_pair(nxt, inverse(from_next())),
        along_pair(last, inverse(from_last())),
        *moves,
    )
    back = lax.all_to_all(tiles.reshape(OWNERS, 1, 128), "wide", split_axis=0, concat_axis=0, tiled=True)
    return pick(back.reshape(OWNERS, 128), *own_rows)


EARLY = (
    (0, 0, "self"), (0, 2, "left"), (0, 4, "both"), (0, 5, "both"), (5, 4, "both"),
    (0, 1, "both"), (1, 1, "self"), (0, 3, "left"), (1, 2, "left"), (1, 3, "left"),
    (1, 4, "both"), (1, 5, "both"), (3, 4, "both"), (3, 5, "both"),
)
LATE = ((5, 6, "both"), (7, 4, "both"), (1, 6, "both"), (1, 7, "both"), (7, 6, "both"))


def match(a, second, tails):
    own_a, sib_a, next_a, last_a = a
    own_b, sib_b, next_b, last_b = second
    width = CHUNK + lanes(own_b.shape[0])
    own, sib, nxt, last = pairs(
        EARLY,
        (own_a, own_b, sib_a, sib_b, next_a, last_a),
        (),
        ((0, 1, ()), (2, 3, ()), (4, None, ()), (5, None, ())),
        (),
        width,
        "early",
    )
    sib = along_pair(sib, swap_cores())
    return pairs(
        LATE,
        (own_a, own_b, sib_a, sib_b, next_a, last_a, next_b, last_b),
        (own, sib, nxt, last),
        ((0, 1, (0, 1)), (4, 6, (2,)), (5, 7, (3,))),
        tails,
        width,
        "late",
    )


def neighbours(block):
    return (
        block,
        along_pair(block, swap_cores()),
        along_pair(block, from_next()),
        along_pair(block, from_last()),
    )


def exchange(embeddings, ids):
    first, unit, meta = prep(embeddings, ids)
    own_a = to_owners(first)
    own_a, unit = lax.optimization_barrier((own_a, unit))
    a = neighbours(own_a)
    return a, to_owners(rest(unit, meta)), meta


def whole(embeddings, ids, a, own_b):
    _, _, meta = prep(embeddings, ids)
    best = match(a, neighbours(own_b), ())
    return give_back(*best, (meta, ranks_of(meta)))[0]


def per_device(embeddings, cluster_ids):
    ids = cluster_ids.reshape(1, -1)
    a, own_b, meta = exchange(embeddings, ids)
    packed, spot = pack(own_b)
    packed, spot, meta, *a = lax.optimization_barrier((packed, spot, meta, *a))
    best = match(a, neighbours(packed), (1, 3, 6, 7))
    value, flag = give_back(*best, (meta, ranks_of(meta)), *moves_of(spot))
    return lax.cond(
        flag.reshape(()) != 0, lambda: whole(embeddings, ids, a, own_b), lambda: value
    ).reshape(-1)


def solution(mesh):
    in_specs = (P(("wide", "pair"), None), P(("wide", "pair")))
    out_specs = P(("wide", "pair"))
    return jax.shard_map(
        per_device, mesh=mesh, in_specs=in_specs, out_specs=out_specs, check_vma=False
    )
```

```python
import functools

import jax
import jax.numpy as jnp
from jax import lax
from jax.experimental import pallas as pl
from jax.experimental.pallas import tpu as pltpu
from jax.sharding import PartitionSpec as P

EPSILON = 1e-06
OWNERS = 16
CAP = 64
HALF = CAP // 2
CHUNK = OWNERS * HALF
SHORT = 208
LOW = -1e30
MARK = 2.0
F32 = jnp.float32
BF16 = jnp.bfloat16


def params():
    return pltpu.CompilerParams(vmem_limit_bytes=24 * 1024 * 1024)


def cost(flops, bytes_accessed):
    return pl.CostEstimate(flops=flops, bytes_accessed=bytes_accessed, transcendentals=0)


def iota(shape, dim):
    return lax.broadcasted_iota(jnp.int32, shape, dim)


def marked(head):
    return head.astype(F32)[:, 0:1] > 1.5


def place(half, unit, ids, rank, out_ref):
    rows = unit.shape[0]
    inside = (rank >= half * HALF) & (rank < (half + 1) * HALF)
    slot = jnp.where(inside, ids * HALF + rank - half * HALF, -1)
    onehot = (iota((CHUNK, rows), 0) == slot).astype(BF16)
    moved = jnp.dot(onehot, unit, preferred_element_type=F32)
    taken = jnp.dot(onehot, jnp.ones((rows, 128), BF16), preferred_element_type=F32)
    out_ref[...] = moved.astype(BF16)
    mark = jnp.where(iota((CHUNK, 128), 1) == 0, MARK * (1.0 - taken), 0.0)
    out_ref[:, 0:128] = (moved[:, 0:128] + mark).astype(BF16)


def prep_kernel(x_hbm, ids_hbm, first_ref, unit_ref, meta_ref, x_ref, ids_ref, sems):
    rows = x_ref.shape[0]
    parts = 8
    step = rows // parts
    copies = [pltpu.make_async_copy(ids_hbm, ids_ref, sems.at[parts])]
    for i in range(parts):
        at = pl.ds(i * step, step)
        copies.append(pltpu.make_async_copy(x_hbm.at[at], x_ref.at[at], sems.at[i]))
    for copy in copies:
        copy.start()
    copies[0].wait()
    ids = ids_ref[...]
    onehot = iota((OWNERS, rows), 0) == ids
    upto = (iota((rows, rows), 0) <= iota((rows, rows), 1)).astype(BF16)
    counts = jnp.dot(onehot.astype(BF16), upto, preferred_element_type=F32)
    rank = jnp.sum(jnp.where(onehot, counts, 0.0), axis=0, keepdims=True).astype(jnp.int32) - 1
    meta_ref[...] = jnp.where(iota((8, rows), 0) == 0, ids, rank)
    groups = 2
    for i in range(groups):
        for j in range(parts // groups):
            copies[1 + i * (parts // groups) + j].wait()
        at = pl.ds(i * (rows // groups), rows // groups)
        x = x_ref[at, :]
        scale = lax.rsqrt(jnp.sum(x * x, axis=1, keepdims=True) + EPSILON)
        unit_ref[at, :] = (x * scale).astype(BF16)
    place(0, unit_ref[...], ids, rank, first_ref)


def prep(embeddings, ids):
    rows, width = embeddings.shape
    return pl.pallas_call(
        prep_kernel,
        in_specs=[pl.BlockSpec(memory_space=pltpu.HBM)] * 2,
        out_shape=(
            jax.ShapeDtypeStruct((CHUNK, width), BF16),
            jax.ShapeDtypeStruct((rows, width), BF16),
            jax.ShapeDtypeStruct((8, rows), jnp.int32),
        ),
        scratch_shapes=[
            pltpu.VMEM((rows, width), F32),
            pltpu.VMEM((1, rows), jnp.int32),
            pltpu.SemaphoreType.DMA((9,)),
        ],
        compiler_params=params(),
        cost_estimate=cost(2 * CHUNK * rows * width, 8 * rows * width),
        name="prep",
    )(embeddings, ids)


def rest_kernel(unit_ref, meta_ref, second_ref, ranks_ref):
    ranks_ref[...] = (iota(ranks_ref.shape, 0) == meta_ref[1:2, :]).astype(BF16)
    place(1, unit_ref[...], meta_ref[0:1, :], meta_ref[1:2, :], second_ref)


def rest(unit, meta):
    rows, width = unit.shape
    return pl.pallas_call(
        rest_kernel,
        out_shape=(
            jax.ShapeDtypeStruct((CHUNK, width), BF16),
            jax.ShapeDtypeStruct((128, rows), BF16),
        ),
        compiler_params=params(),
        cost_estimate=cost(2 * CHUNK * rows * width, 4 * rows * width),
        name="rest",
    )(unit, meta)


def pack_kernel(block_ref, packed_ref, source_ref, spread_ref):
    rows = block_ref.shape[0]
    full = jnp.where(marked(block_ref[:, 0:128]), 0.0, 1.0)
    full = jnp.transpose(jnp.broadcast_to(full, (rows, 128)))[0:8, :]
    upto = (iota((rows, rows), 0) <= iota((rows, rows), 1)).astype(BF16)
    count = jnp.dot(full.astype(BF16), upto, preferred_element_type=F32)
    spot = jnp.where(full > 0.5, count - 1.0, -1.0).astype(jnp.int32)
    wide = (iota((lanes(SHORT), rows), 0) == spot[0:1, :]).astype(BF16)
    source = (iota((OWNERS, rows), 1) // HALF == iota((OWNERS, rows), 0)).astype(BF16)
    source_ref[...] = lax.dot_general(
        source, wide, (((1,), (1,)), ((), ())), preferred_element_type=F32
    )
    lane = (iota((rows, 128), 0) % HALF + HALF == iota((rows, 128), 1)).astype(BF16)
    spread_ref[...] = jnp.dot(wide, lane, preferred_element_type=F32).astype(BF16)
    onehot = wide[0:SHORT, :]
    moved = jnp.dot(onehot, block_ref[...], preferred_element_type=F32)
    taken = jnp.dot(onehot, jnp.ones((rows, 128), BF16), preferred_element_type=F32)
    packed_ref[...] = moved.astype(BF16)
    mark = jnp.where(iota((SHORT, 128), 1) == 0, MARK * (1.0 - taken), 0.0)
    packed_ref[:, 0:128] = (moved[:, 0:128] + mark).astype(BF16)


def pack(block):
    rows, width = block.shape
    return pl.pallas_call(
        pack_kernel,
        out_shape=(
            jax.ShapeDtypeStruct((SHORT, width), BF16),
            jax.ShapeDtypeStruct((OWNERS, lanes(SHORT)), F32),
            jax.ShapeDtypeStruct((lanes(SHORT), 128), BF16),
        ),
        compiler_params=params(),
        cost_estimate=cost(2 * SHORT * rows * width, 4 * rows * width),
        name="pack",
    )(block)


def lanes(rows):
    return -(-rows // 128) * 128


def pair_kernel(units, n_blocks, n_before, wanted, tails, *refs):
    blocks = refs[:n_blocks]
    before = refs[n_blocks : n_blocks + n_before]
    outs = refs[n_blocks + n_before : n_blocks + n_before + len(wanted)]
    lane_bias, row_bias, over_lanes, over_rows = refs[n_blocks + n_before + len(wanted) :]
    lefts = sorted({left for left, _, _ in units})
    rights = sorted({right for _, right, mode in units if mode == "both"})
    for b in sorted({b for unit in units for b in unit[0:2]}):
        rows = blocks[b].shape[0]
        bias = jnp.where(marked(blocks[b][:, 0:128]), LOW, 0.0)
        lane_bias[b, 0:rows] = jnp.broadcast_to(bias, (rows, 128))
        if any(b == right for _, right, _ in units):
            turned = jnp.transpose(lane_bias[b, 0 : lanes(rows)])
            row_bias[b, :, 0 : lanes(rows)] = turned[0:8, :]
        if b in lefts:
            over_lanes[b, 0 : lanes(rows)] = jnp.full((lanes(rows), 128), LOW, F32)
        if b in rights:
            over_rows[b, :, 0 : lanes(rows)] = jnp.full((8, lanes(rows)), LOW, F32)
    for left, right, mode in units:
        n_left, n_right = blocks[left].shape[0], blocks[right].shape[0]
        scores = lax.dot_general(
            blocks[left][...], blocks[right][...], (((1,), (1,)), ((), ())), preferred_element_type=F32
        )
        valid = scores + row_bias[right, 0:1, 0:n_right]
        if mode == "self":
            valid = jnp.where(iota(scores.shape, 0) == iota(scores.shape, 1), LOW, valid)
        best = over_lanes[left, 0:n_left]
        whole_groups = n_right // 128 * 128
        for g in range(0, whole_groups, 128):
            best = jnp.maximum(best, valid[:, g : g + 128])
        over_lanes[left, 0:n_left] = best
        if whole_groups < n_right:
            some = n_right - whole_groups
            best = jnp.maximum(over_lanes[left, 0:n_left, 0:some], valid[:, whole_groups:])
            over_lanes[left, 0:n_left, 0:some] = best
        if mode == "both":
            bias = lane_bias[left, 0:n_left]
            for g in range(0, n_right, 128):
                end = min(g + 128, n_right)
                part = scores[:, g:end] + bias[:, 0 : end - g]
                part = jnp.max(part.reshape(n_left // 8, 8, end - g), axis=0)
                over_rows[right, :, g:end] = jnp.maximum(over_rows[right, :, g:end], part)
    flag = jnp.zeros((1, 128), F32)
    for b in tails:
        end = blocks[b].shape[0]
        last = blocks[b][end - 16 : end, 0:128].astype(F32)[15:16, 0:1]
        flag = jnp.maximum(flag, jnp.where(last > 1.5, 0.0, 1.0))
    for (first, second, earlier), out in zip(wanted, outs):
        for b, at, n in ((first, 0, CHUNK), (second, CHUNK, out.shape[1] - CHUNK - 128)):
            part = jnp.full((1, n), LOW, F32)
            if b in lefts:
                part = jnp.max(jnp.transpose(over_lanes[b, 0:n]), axis=0, keepdims=True)
            if b in rights:
                part = jnp.maximum(part, jnp.max(over_rows[b, :, 0:n], axis=0, keepdims=True))
            for e in earlier:
                part = jnp.maximum(part, before[e][:, at : at + n])
            out[:, at : at + n] = part
        out[:, out.shape[1] - 128 :] = flag


def pairs(units, blocks, before, wanted, tails, width, name):
    n = len(blocks)
    rows, depth = blocks[0].shape
    work = sum(blocks[a].shape[0] * blocks[b].shape[0] for a, b, _ in units)
    return pl.pallas_call(
        functools.partial(pair_kernel, units, n, len(before), wanted, tails),
        out_shape=tuple(jax.ShapeDtypeStruct((1, width + 128), F32) for _ in wanted),
        scratch_shapes=[
            pltpu.VMEM((n, rows, 128), F32),
            pltpu.VMEM((n, 8, rows), F32),
            pltpu.VMEM((n, rows, 128), F32),
            pltpu.VMEM((n, 8, rows), F32),
        ],
        compiler_params=params(),
        cost_estimate=cost(2 * work * depth, 2 * n * rows * depth),
        name=name,
    )(*blocks, *before)


def three_parts(value):
    parts = []
    for _ in range(3):
        part = value.astype(BF16).astype(F32)
        value = value - part
        parts.append(part)
    return jnp.concatenate(parts, axis=0).astype(BF16)


def join_kernel(packed, own_ref, a_ref, b_ref, *rest):
    best = jnp.maximum(jnp.maximum(own_ref[...], a_ref[...]), jnp.maximum(b_ref[...], -1.0))
    out_ref = rest[-1]
    second = best[:, CHUNK:-128]
    if packed:
        source_ref, spread_ref = rest[:2]
        value = jnp.where(source_ref[...] > 0.5, second, 0.0)
        moved = jnp.dot(three_parts(value), spread_ref[...], preferred_element_type=F32)
        out_ref[...] = moved[0:OWNERS] + moved[OWNERS : 2 * OWNERS] + moved[2 * OWNERS :]
    for source in range(OWNERS):
        at = source * HALF
        row = slice(source, source + 1)
        out_ref[row, 0:HALF] = best[:, at : at + HALF]
        if not packed:
            out_ref[row, HALF:CAP] = second[:, at : at + HALF]
        out_ref[row, CAP:128] = best[:, -CAP:]


def join(own, a, b, *moves):
    return pl.pallas_call(
        functools.partial(join_kernel, bool(moves)),
        out_shape=pltpu.VMEM((OWNERS, 128), F32),
        compiler_params=params(),
        name="join",
    )(own, a, b, *moves)


def pick_kernel(back_ref, meta_ref, ranks_ref, out_ref, flag_ref):
    rows = meta_ref.shape[1]
    tiles = back_ref[...]
    moved = jnp.dot(three_parts(tiles), ranks_ref[...], preferred_element_type=F32)
    moved = moved[0:OWNERS] + moved[OWNERS : 2 * OWNERS] + moved[2 * OWNERS :]
    mine = iota((OWNERS, rows), 0) == meta_ref[0:1, :]
    out_ref[...] = jnp.sum(jnp.where(mine, moved, 0.0), axis=0, keepdims=True)
    flag_ref[0, 0] = (jnp.max(tiles[:, CAP:]) > 0.5).astype(jnp.int32)


def pick(back, meta, ranks):
    return pl.pallas_call(
        pick_kernel,
        out_shape=(
            jax.ShapeDtypeStruct((1, meta.shape[1]), F32),
            pltpu.SMEM((1, 1), jnp.int32),
        ),
        out_specs=(
            pl.BlockSpec(memory_space=pltpu.VMEM),
            pl.BlockSpec(memory_space=pltpu.SMEM),
        ),
        compiler_params=params(),
        name="pick",
    )(back, meta, ranks)


def swap_cores():
    return [(2 * z + k, 2 * z + 1 - k) for z in range(4) for k in range(2)]


LAST_CROSS = (0, 1, 1, 1)


def from_next():
    return [
        (2 * ((z + 1) % 4) + (k ^ 1 ^ LAST_CROSS[(z + 1) % 4]), 2 * z + k)
        for z in range(4)
        for k in range(2)
    ]


def from_last():
    return [(2 * ((z + 3) % 4) + (k ^ LAST_CROSS[z]), 2 * z + k) for z in range(4) for k in range(2)]


def inverse(perm):
    return [(b, a) for a, b in perm]


def to_owners(block):
    shape = block.shape
    block = block.reshape(OWNERS, HALF, shape[1])
    return lax.all_to_all(block, "wide", split_axis=0, concat_axis=0, tiled=True).reshape(shape)


def along_pair(block, perm):
    return lax.ppermute(block, "pair", perm)


def give_back(own, nxt, last, own_rows, *moves):
    tiles = join(
        own,
        along_pair(nxt, inverse(from_next())),
        along_pair(last, inverse(from_last())),
        *moves,
    )
    back = lax.all_to_all(tiles.reshape(OWNERS, 1, 128), "wide", split_axis=0, concat_axis=0, tiled=True)
    return pick(back.reshape(OWNERS, 128), *own_rows)


EARLY = (
    (0, 0, "self"), (0, 2, "left"), (0, 4, "both"), (0, 5, "both"), (5, 4, "both"),
    (0, 1, "both"), (1, 1, "self"), (0, 3, "left"), (1, 2, "left"), (1, 3, "left"),
    (1, 4, "both"), (1, 5, "both"), (3, 4, "both"), (3, 5, "both"),
)
LATE = ((5, 6, "both"), (7, 4, "both"), (1, 6, "both"), (1, 7, "both"), (7, 6, "both"))


def match(a, second, tails):
    own_a, sib_a, next_a, last_a = a
    own_b, sib_b, next_b, last_b = second
    width = CHUNK + lanes(own_b.shape[0])
    own, sib, nxt, last = pairs(
        EARLY,
        (own_a, own_b, sib_a, sib_b, next_a, last_a),
        (),
        ((0, 1, ()), (2, 3, ()), (4, None, ()), (5, None, ())),
        (),
        width,
        "early",
    )
    sib = along_pair(sib, swap_cores())
    return pairs(
        LATE,
        (own_a, own_b, sib_a, sib_b, next_a, last_a, next_b, last_b),
        (own, sib, nxt, last),
        ((0, 1, (0, 1)), (4, 6, (2,)), (5, 7, (3,))),
        tails,
        width,
        "late",
    )


def neighbours(block):
    return (
        block,
        along_pair(block, swap_cores()),
        along_pair(block, from_next()),
        along_pair(block, from_last()),
    )


def exchange(embeddings, ids):
    first, unit, meta = prep(embeddings, ids)
    own_a = to_owners(first)
    own_a, unit = lax.optimization_barrier((own_a, unit))
    a = neighbours(own_a)
    second, ranks = rest(unit, meta)
    return a, to_owners(second), (meta, ranks)


def whole(embeddings, ids, a, own_b):
    _, unit, meta = prep(embeddings, ids)
    _, ranks = rest(unit, meta)
    best = match(a, neighbours(own_b), ())
    return give_back(*best, (meta, ranks))[0]


def per_device(embeddings, cluster_ids):
    ids = cluster_ids.reshape(1, -1)
    a, own_b, own_rows = exchange(embeddings, ids)
    packed, *moves = pack(own_b)
    packed, *a = lax.optimization_barrier((packed, *a))
    best = match(a, neighbours(packed), (1, 3, 6, 7))
    value, flag = give_back(*best, own_rows, *moves)
    return lax.cond(
        flag.reshape(()) != 0, lambda: whole(embeddings, ids, a, own_b), lambda: value
    ).reshape(-1)


def solution(mesh):
    in_specs = (P(("wide", "pair"), None), P(("wide", "pair")))
    out_specs = P(("wide", "pair"))
    return jax.shard_map(
        per_device, mesh=mesh, in_specs=in_specs, out_specs=out_specs, check_vma=False
    )
```
